32 devices in a mesh: groups: 2 (over x), dp: 2 (over core), tensor: 8 (over z, y).
Axes of the slice: x: 2, y: 2, z: 4, core: 2. Of those that a mesh axis runs over, the one named last changes fastest.
Arguments:
- reward_hidden: bfloat16 [32, 256, 8192], P(('groups', 'dp'), None, 'tensor'), parts along dimension 0, may hold values from -6 to 6
- reward_gain: float32 [8192], P('tensor'), may hold values from 0.5 to 1.5
- reward_head: float32 [8192], P('tensor'), may hold values from -1 to 1
- decode_inputs: bfloat16 [2, 32, 8192], P(None, ('groups', 'dp'), 'tensor'), parts along dimension 1, may hold values from -6 to 6
- attn_gain: float32 [8192], replicated, may hold values from 0.5 to 1.5
- w_query: bfloat16 [8192, 8192], P(None, 'tensor'), may hold values from -0.0625 to 0.0625
- w_keyval: bfloat16 [8192, 2048], P(None, 'tensor'), may hold values from -0.0625 to 0.0625
- w_out: bfloat16 [8192, 8192], P('tensor'), may hold values from -3 to 3
- cache_keys: bfloat16 [32, 2048, 1024], P(('groups', 'dp'), 'tensor'), parts along dimension 0, may hold values from -720 to 720
- cache_values: bfloat16 [32, 2048, 1024], P(('groups', 'dp'), 'tensor'), parts along dimension 0, may hold values from -6 to 6
- lengths: int32 [32], P('groups'), parts along dimension 0, may hold values from 512 to 2048
- slot_map: int32 [32], P('groups'), parts along dimension 0, may hold values from 0 to 15, as said below
Outputs:
- reward: float32 [32], P(('groups', 'dp')), parts along dimension 0
- decoded: bfloat16 [2, 32, 8192], P(None, ('groups', 'dp'), 'tensor'), parts along dimension 1
The draws below stay inside these ranges and needn't reach their ends.
There are 2 independent parts, one for each index of `groups`. The reference program is written for one: setup_inputs(seed, part) draws one part's arguments, and reference() takes and returns one part's arrays. A program takes and returns all parts, laid end to end along the dimension named above; an argument that names none is the same for every part. Nothing has to cross between parts.
Inputs may be any that keep to these rules, and one draw needn't show every extreme that they name: `slot_map`: each aligned block of 8 slots holds exactly 4 survivors, which map to themselves; every other slot maps to a survivor, and every survivor is named by exactly one other slot.
All inputs are finite; a program needn't handle non-finite values.
Results may differ from the reference program's by a relative error of at most 0.0055.
The reference program's roundings to bfloat16 on the way (of `normed`, `query`, `keyval`, `weights` and `attended`) count: a program that leaves them out, or rounds other values in their place, can miss the bound.
Values may be sent and summed in bfloat16 or wider, within the bound.
A program may use at most 128 MiB of HBM per device.

```python
import jax
import jax.numpy as jnp
from jax import lax

D = 8192
QH = 64
KVH = 8
HD = 128
SPAN = 256
CACHE_LEN = 2048
RESP_DEV = 8
STEPS = 2
RESP = 16
BLOCK_POS = 256
N_TENSOR = 8


def draw_lengths(key, part):
    drawn = jax.random.randint(jax.random.fold_in(key, 11), (RESP,), CACHE_LEN // 4, CACHE_LEN + 1)
    return drawn.at[0].set(CACHE_LEN).astype(jnp.int32)


def draw_slot_map(key, part):
    blocks = RESP // RESP_DEV
    half = RESP_DEV // 2
    block_keys = jax.random.split(jax.random.fold_in(key, 23), blocks)
    orders = jax.vmap(lambda k: jax.random.permutation(k, RESP_DEV))(block_keys)
    offsets = (jnp.arange(blocks) * RESP_DEV)[:, None]
    kept = (orders[:, :half] + offsets).reshape(-1)
    freed = (orders[:, half:] + offsets).reshape(-1)
    match = jax.random.permutation(jax.random.fold_in(key, 37), RESP // 2)
    result = jnp.arange(RESP).at[freed].set(kept[match])
    return result.astype(jnp.int32)


def draw_cache_keys(key, part):
    base = jax.random.normal(jax.random.fold_in(key, 41), (RESP, CACHE_LEN, KVH, HD), jnp.float32)
    base = jnp.clip(base, -6.0, 6.0)
    return base.reshape(RESP, CACHE_LEN, KVH * HD).astype(jnp.bfloat16)


def block_levels(rng, shape, cuts, low, high):
    def one(dim, blocks):
        steps = jax.random.uniform(jax.random.fold_in(jax.random.fold_in(rng, 6), dim), (blocks,), jnp.float32, low / len(cuts), high / len(cuts))
        return jnp.repeat(jnp.exp(steps), shape[dim] // blocks).reshape((-1,) + (1,) * (len(shape) - dim - 1))

    factor_of = one(*cuts[0])
    for cut in cuts[1:]:
        factor_of = factor_of * one(*cut)
    return factor_of


def centred(stream_key, dims, spread, limit, pieces=(), kind=jnp.bfloat16):
    values = spread * jax.random.normal(stream_key, dims, jnp.float32)
    if pieces:
        values = values * block_levels(stream_key, dims, pieces, -0.22, 0.18)
    return jnp.clip(values, -limit, limit).astype(kind)


def setup_inputs(seed: int = 0, part: int = 0) -> dict:
    key_of = jax.random.split(jax.random.key(seed), 13)
    own_keys = jax.random.split(jax.random.fold_in(key_of[12], part), 13)
    reward_hidden = centred(own_keys[0], (RESP, SPAN, D), 1.0, 6.0, ((0, 2), (2, 8)))
    reward_gain = jnp.clip(1.0 + 0.1 * jax.random.normal(key_of[1], (D,), jnp.float32), 0.5, 1.5)
    reward_head = centred(key_of[2], (D,), (D // SPAN) ** -0.5, 1.0, ((0, 8),), jnp.float32)
    decode_inputs = centred(own_keys[3], (STEPS, RESP, D), 1.0, 6.0, ((1, 2), (2, 8)))
    attn_gain = jnp.clip(1.0 + 0.1 * jax.random.normal(key_of[4], (D,), jnp.float32), 0.5, 1.5)
    w_query = centred(key_of[5], (D, QH * HD), D ** -0.5, 0.0625, ((1, 8),))
    w_keyval = centred(key_of[6], (D, 2 * KVH * HD), D ** -0.5, 0.0625, ((1, 8),))
    w_out = centred(key_of[7], (QH * HD, D), (QH * HD // CACHE_LEN) ** -0.5, 3.0, ((0, 8),))
    cache_keys = draw_cache_keys(jax.random.fold_in(jax.random.fold_in(key_of[12], part), 71), part)
    cache_values = centred(own_keys[9], (RESP, CACHE_LEN, KVH * HD), 1.0, 6.0, ((0, 2), (1, 8)))
    lengths = draw_lengths(jax.random.fold_in(jax.random.fold_in(key_of[12], part), 71), part)
    slot_map = draw_slot_map(jax.random.fold_in(jax.random.fold_in(key_of[12], part), 71), part)
    return dict(reward_hidden=reward_hidden, reward_gain=reward_gain, reward_head=reward_head, decode_inputs=decode_inputs, attn_gain=attn_gain, w_query=w_query, w_keyval=w_keyval, w_out=w_out, cache_keys=cache_keys, cache_values=cache_values, lengths=lengths, slot_map=slot_map)


EPS = 1e-05
NEG = -1e+30

def reference(reward_hidden, reward_gain, reward_head, decode_inputs, attn_gain, w_query, w_keyval, w_out, cache_keys, cache_values, lengths, slot_map):
    hidden = reward_hidden.astype(jnp.float32)
    squares = lax.optimization_barrier(jnp.sum(hidden * hidden, axis=-1))
    head_dot = lax.optimization_barrier(jnp.sum(hidden * (reward_gain * reward_head), axis=-1))
    reward = lax.optimization_barrier(jnp.mean(head_dot * lax.rsqrt(squares / D + EPS), axis=-1))
    keys_now = jnp.take(cache_keys, slot_map, axis=0)
    values_now = jnp.take(cache_values, slot_map, axis=0)
    live = jnp.take(lengths, slot_map, axis=0)
    slots = keys_now.shape[0]
    group = QH // KVH
    keys5 = keys_now.reshape(slots, N_TENSOR, BLOCK_POS, KVH, HD).astype(jnp.float32)
    values5 = values_now.reshape(slots, N_TENSOR, BLOCK_POS, KVH, HD).astype(jnp.float32)
    places = jnp.arange(CACHE_LEN).reshape(N_TENSOR, BLOCK_POS)
    valid = (places[None, :, :] < live[:, None, None])[:, None, None, :, :]
    scale = HD ** (-0.5)
    new_keys = []
    new_values = []
    outputs = []
    for step in range(STEPS):
        xf = decode_inputs[step].astype(jnp.float32)
        normed = (xf * lax.rsqrt(lax.optimization_barrier(jnp.mean(xf * xf, axis=-1, keepdims=True)) + EPS) * attn_gain).astype(jnp.bfloat16)
        query = jnp.dot(normed, w_query, preferred_element_type=jnp.float32).astype(jnp.bfloat16)
        query = query.reshape(slots, KVH, group, HD).astype(jnp.float32)
        keyval = jnp.dot(normed, w_keyval, preferred_element_type=jnp.float32).astype(jnp.bfloat16).reshape(slots, 2, KVH, HD)
        new_keys.append(keyval[:, 0].astype(jnp.float32))
        new_values.append(keyval[:, 1].astype(jnp.float32))
        fresh_k = jnp.stack(new_keys, axis=1)
        fresh_v = jnp.stack(new_values, axis=1)
        scores = jnp.einsum('rkgd,rbwkd->rkgbw', query, keys5) * scale
        scores = jnp.where(valid, scores, NEG)
        block_max = lax.optimization_barrier(jnp.max(scores, axis=-1))
        expo = jnp.where(valid, jnp.exp(scores - block_max[..., None]), 0.0)
        block_total = lax.optimization_barrier(jnp.sum(expo, axis=-1))
        weights = expo.astype(jnp.bfloat16).astype(jnp.float32)
        block_acc = jnp.einsum('rkgbw,rbwkd->rkgbd', weights, values5)
        recent = jnp.einsum('rkgd,rjkd->rkgj', query, fresh_k) * scale
        recent_max = lax.optimization_barrier(jnp.max(recent, axis=-1))
        recent_exp = jnp.exp(recent - recent_max[..., None])
        recent_total = lax.optimization_barrier(jnp.sum(recent_exp, axis=-1))
        recent_w = recent_exp.astype(jnp.bfloat16).astype(jnp.float32)
        recent_acc = jnp.einsum('rkgj,rjkd->rkgd', recent_w, fresh_v)
        top = jnp.maximum(lax.optimization_barrier(jnp.max(block_max, axis=-1)), recent_max)
        block_scale = jnp.exp(block_max - top[..., None])
        recent_scale = jnp.exp(recent_max - top)
        total = lax.optimization_barrier(jnp.sum(block_scale * block_total, axis=-1)) + recent_scale * recent_total
        acc = lax.optimization_barrier(jnp.sum(block_scale[..., None] * block_acc, axis=3)) + recent_scale[..., None] * recent_acc
        attended = (acc / total[..., None]).astype(jnp.bfloat16).reshape(slots, QH * HD)
        outputs.append(jnp.dot(attended, w_out, preferred_element_type=jnp.float32).astype(jnp.bfloat16))
    return (reward, jnp.stack(outputs, axis=0))
```

```python
import functools

import jax
import jax.numpy as jnp
from jax import lax
from jax.experimental import pallas as pl
from jax.experimental.pallas import tpu as pltpu
from jax.sharding import PartitionSpec as P

D = 8192
QH = 64
KVH = 8
HD = 128
STEPS = 2


EPS = 1e-05
NEG = -1e30


def fold_sources(parts):
    maxima, totals, sums = parts
    top = jnp.max(maxima, axis=0)
    factor = jnp.exp(maxima - top[None])
    return (top, jnp.sum(factor * totals, axis=0), jnp.sum(factor[..., None] * sums, axis=0))


def local(
    reward_hidden,
    reward_gain,
    reward_head,
    decode_inputs,
    attn_gain,
    w_query,
    w_keyval,
    w_out,
    cache_keys,
    cache_values,
    lengths,
    slot_map,
):
    hidden = reward_hidden.astype(jnp.float32)
    squares = jnp.sum(hidden * hidden, axis=-1)
    head_dot = jnp.sum(hidden * (reward_gain * reward_head), axis=-1)
    squares, head_dot = lax.psum((squares, head_dot), "tensor")
    reward = jnp.mean(head_dot * lax.rsqrt(squares / D + EPS), axis=-1)
    rows = cache_keys.shape[0]
    width = cache_keys.shape[1]
    base = lax.axis_index("dp") * rows
    mine = lax.dynamic_slice_in_dim(slot_map, base, rows)
    every_k, every_v = (
        lax.all_gather(cache_keys, "dp", axis=0, tiled=True),
        lax.all_gather(cache_values, "dp", axis=0, tiled=True),
    )
    keys_now = jnp.take(every_k, mine, axis=0)
    values_now = jnp.take(every_v, mine, axis=0)
    live = jnp.take(lengths, mine, axis=0)
    group = QH // KVH
    heads_dev = w_query.shape[1] // HD
    keys4 = keys_now.reshape(rows, width, KVH, HD)
    values4 = values_now.reshape(rows, width, KVH, HD)
    positions = lax.axis_index("tensor") * width + jnp.arange(width)
    valid = (positions[None, :] < live[:, None])[:, None, None, :]
    head_start = lax.axis_index("tensor") * heads_dev
    kv_index = (head_start + jnp.arange(heads_dev)) // group
    scale = HD ** (-0.5)
    new_keys = []
    new_values = []
    outputs = []
    for step in range(STEPS):
        whole = lax.all_gather(decode_inputs[step], "tensor", axis=1, tiled=True).astype(
            jnp.float32
        )
        normed = (
            whole * lax.rsqrt(jnp.mean(whole * whole, axis=-1, keepdims=True) + EPS) * attn_gain
        ).astype(jnp.bfloat16)
        query_part = jnp.dot(normed, w_query, preferred_element_type=jnp.float32).astype(
            jnp.bfloat16
        )
        kv_part = jnp.dot(normed, w_keyval, preferred_element_type=jnp.float32).astype(jnp.bfloat16)
        query_all, keyval = (
            lax.all_gather(query_part, "tensor", axis=1, tiled=True),
            lax.all_gather(kv_part, "tensor", axis=1, tiled=True),
        )
        query = query_all.reshape(rows, KVH, group, HD)
        keyval = keyval.reshape(rows, 2, KVH, HD)
        new_keys.append(keyval[:, 0])
        new_values.append(keyval[:, 1])
        scores = (
            jnp.einsum("rkgd,rwkd->rkgw", query, keys4, preferred_element_type=jnp.float32) * scale
        )
        scores = jnp.where(valid, scores, NEG)
        block_max = jnp.max(scores, axis=-1)
        expo = jnp.where(valid, jnp.exp(scores - block_max[..., None]), 0.0)
        block_total = jnp.sum(expo, axis=-1).reshape(rows, QH)
        block_acc = jnp.einsum(
            "rkgw,rwkd->rkgd",
            expo.astype(jnp.bfloat16),
            values4,
            preferred_element_type=jnp.float32,
        )
        block_acc = block_acc.reshape(rows, QH, HD)
        block_max = block_max.reshape(rows, QH)
        cache_top, cache_total, cache_acc = fold_sources(
            (
                lax.all_to_all(block_max[None], "tensor", split_axis=2, concat_axis=0, tiled=True),
                lax.all_to_all(
                    block_total[None], "tensor", split_axis=2, concat_axis=0, tiled=True
                ),
                lax.all_to_all(block_acc[None], "tensor", split_axis=2, concat_axis=0, tiled=True),
            )
        )
        query_own = query_part.reshape(rows, heads_dev, HD)
        fresh_k = jnp.take(jnp.stack(new_keys, axis=1), kv_index, axis=2)
        fresh_v = jnp.take(jnp.stack(new_values, axis=1), kv_index, axis=2)
        recent = (
            jnp.einsum("rhd,rjhd->rhj", query_own, fresh_k, preferred_element_type=jnp.float32)
            * scale
        )
        recent_max = jnp.max(recent, axis=-1)
        recent_exp = jnp.exp(recent - recent_max[..., None])
        recent_total = jnp.sum(recent_exp, axis=-1)
        recent_acc = jnp.einsum(
            "rhj,rjhd->rhd",
            recent_exp.astype(jnp.bfloat16),
            fresh_v,
            preferred_element_type=jnp.float32,
        )
        top = jnp.maximum(cache_top, recent_max)
        cache_factor = jnp.exp(cache_top - top)
        recent_factor = jnp.exp(recent_max - top)
        total = cache_factor * cache_total + recent_factor * recent_total
        acc = cache_factor[..., None] * cache_acc + recent_factor[..., None] * recent_acc
        attended = (acc / total[..., None]).astype(jnp.bfloat16).reshape(rows, heads_dev * HD)
        partial_out = jnp.dot(attended, w_out, preferred_element_type=jnp.float32)
        summed = lax.psum_scatter(partial_out, "tensor", scatter_dimension=1, tiled=True)
        outputs.append(summed.astype(jnp.bfloat16))
    return (reward, jnp.stack(outputs, axis=0))


def dot(a, b, dims=(((1,), (0,)), ((), ()))):
    return lax.dot_general(a, b, dims, preferred_element_type=jnp.float32)


def iota(shape, dim):
    return lax.broadcasted_iota(jnp.int32, shape, dim)


def kernel(
    n, ndp, rows, span, width,
    map_ref, len_ref, x_hbm, gain_ref, rgain_ref, rhead_ref, rh_hbm, wq_hbm, wkv_hbm, wo_hbm, k_hbm, v_hbm,
    reward_ref, out_ref,
    rh, wq, wkv, wo, kbuf, vbuf,
    xall, xg, normed, kvg, qf, qtmp, qsend, qg, accs, accr, mls, mlr, fac, att, osend, orecv, fin, rw,
    loc, xds, xdr, xs, xr, rs, rr, kvs, kvr, qs, qr, as_, ar, ms, mr, os_, or_, fds, fdr,
):
    me = lax.axis_index("tensor")
    dp = lax.axis_index("dp")
    other = 1 - dp
    feat = x_hbm.shape[1]
    pages = rows // 2
    per = 2 * STEPS
    R = rows * STEPS
    group = QH // KVH
    unit = group * per
    total_rows = pages * unit
    scale = HD ** (-0.5)

    def peer(k):
        return lax.rem(me + k, n)

    def source(k):
        return lax.rem(me + n - k, n)

    copies = []

    def load(src, dst):
        c = pltpu.make_async_copy(src, dst, loc.at[len(copies)])
        c.start()
        copies.append(c)
        return c

    def load_rows(src, dst, parts):
        step = src.shape[0] // parts
        return [load(src.at[pl.ds(i * step, step)], dst.at[pl.ds(i * step, step)]) for i in range(parts)]

    c_x = load(x_hbm, xall.at[dp])
    c_rh = load_rows(rh_hbm, rh, 2)
    c_wkv = load_rows(wkv_hbm, wkv, 2)
    c_wq = load_rows(wq_hbm, wq, 4)
    c_k = load_rows(k_hbm, kbuf, 2)
    c_v = load_rows(v_hbm, vbuf, 2)
    c_wo = load_rows(wo_hbm, wo, 4)

    barrier = pltpu.get_barrier_semaphore()
    for k in range(1, n):
        pl.semaphore_signal(barrier, inc=1, device_id={"tensor": peer(k)}, device_id_type=pl.DeviceIdType.MESH)
    pl.semaphore_signal(barrier, inc=1, device_id={"dp": other}, device_id_type=pl.DeviceIdType.MESH)

    def to_peer(k, src, dst, ssem, rsem):
        return pltpu.make_async_remote_copy(
            src_ref=src, dst_ref=dst, send_sem=ssem, recv_sem=rsem,
            device_id={"tensor": peer(k)}, device_id_type=pl.DeviceIdType.MESH,
        )

    def to_pair(src, dst, ssem, rsem):
        return pltpu.make_async_remote_copy(
            src_ref=src, dst_ref=dst, send_sem=ssem, recv_sem=rsem,
            device_id={"dp": other}, device_id_type=pl.DeviceIdType.MESH,
        )

    slot = [map_ref[s] for s in range(ndp * rows)]
    first, second = [], []
    for b in range(ndp):
        mine = [jnp.int32(b * rows)] * pages
        count = jnp.int32(0)
        for s in range(b * rows, (b + 1) * rows):
            kept = slot[s] == s
            for i in range(pages):
                mine[i] = jnp.where(kept & (count == i), s, mine[i])
            count = count + jnp.where(kept, 1, 0)
        first.append(mine)
        named = []
        for i in range(pages):
            found = jnp.int32(0)
            for s in range(ndp * rows):
                found = jnp.where((slot[s] == mine[i]) & (mine[i] != s), s, found)
            named.append(found)
        second.append(named)

    def own(lists, i):
        return jnp.where(dp == 0, lists[0][i], lists[1][i])

    first_own = [own(first, i) for i in range(pages)]
    second_own = [own(second, i) for i in range(pages)]

    c_x.wait()
    pl.semaphore_wait(barrier, n)
    pair_x = to_pair(xall.at[dp], xall.at[dp], xds.at[0], xdr.at[0])
    pair_x.start()

    r_i = iota((R, ndp * R), 0)
    c_i = iota((R, ndp * R), 1)
    row_slot = jnp.zeros((R, ndp * R), jnp.int32)
    for i in range(pages):
        row_slot = jnp.where(r_i // STEPS == 2 * i, first_own[i], row_slot)
        row_slot = jnp.where(r_i // STEPS == 2 * i + 1, second_own[i], row_slot)
    col_slot = (c_i // R) * rows + c_i % rows
    pick = (row_slot == col_slot) & (r_i % STEPS == (c_i % R) // rows)
    pick = jnp.where(pick, 1.0, 0.0).astype(jnp.bfloat16)

    pltpu.make_async_remote_copy(
        src_ref=xall.at[other], dst_ref=xall.at[other], send_sem=xds.at[0], recv_sem=xdr.at[0],
        device_id={"dp": other}, device_id_type=pl.DeviceIdType.MESH,
    ).wait_recv()
    chosen = dot(pick, xall[...].reshape(ndp * R, feat))
    xg[me] = chosen.astype(jnp.bfloat16)
    sends = [pair_x]
    for k in range(1, n):
        c = to_peer(k, xg.at[me], xg.at[me], xs.at[k], xr.at[k])
        c.start()
        sends.append(c)

    for c in c_rh:
        c.wait()
    weight = rgain_ref[...] * rhead_ref[...]

    def reward_step(r, carry):
        start = pl.multiple_of(r * span, span)
        square = jnp.zeros((span, 128), jnp.float32)
        head = jnp.zeros((span, 128), jnp.float32)
        for b in range(feat // 128):
            h = rh[pl.ds(start, span), b * 128 : (b + 1) * 128].astype(jnp.float32)
            square = square + h * h
            head = head + h * weight[:, b * 128 : (b + 1) * 128]
        rw[0, 0, pl.ds(r, 1), :] = jnp.sum(jnp.transpose(square), axis=0, keepdims=True)
        rw[0, 1, pl.ds(r, 1), :] = jnp.sum(jnp.transpose(head), axis=0, keepdims=True)
        return carry

    lax.fori_loop(0, rows, reward_step, 0)
    for k in range(1, n):
        c = to_peer(k, rw.at[0], rw.at[k], rs.at[k], rr.at[k])
        c.start()
        sends.append(c)

    mean = jnp.zeros((R, 1), jnp.float32)
    for k in range(n):
        if k:
            s = source(k)
            to_peer(k, xg.at[s], xg.at[s], xs.at[k], xr.at[k]).wait_recv()
    for s in range(n):
        part = xg[s].astype(jnp.float32)
        mean = mean + jnp.sum(part * part, axis=1, keepdims=True)
    factor = lax.rsqrt(mean / (n * feat) + EPS)
    for s in range(n):
        lo, hi = s * feat, (s + 1) * feat
        part = xg[s].astype(jnp.float32)
        normed[:, lo:hi] = (part * factor * gain_ref[:, lo:hi]).astype(jnp.bfloat16)

    for c in c_wkv:
        c.wait()
    kvg[0] = dot(normed[...], wkv[...]).astype(jnp.bfloat16)
    kv_cols = wkv.shape[1]
    for k in range(1, n):
        c = to_peer(k, kvg.at[0], kvg.at[me + 1], kvs.at[k], kvr.at[k])
        c.start()
        sends.append(c)
    for c in c_wq:
        c.wait()
    chunk = 256

    def query_step(c, carry):
        cols = pl.ds(pl.multiple_of(c * chunk, chunk), chunk)
        qf[:, cols] = dot(normed[...], wq[:, cols])
        return carry

    lax.fori_loop(0, group * HD // chunk, query_step, 0)
    for i in range(pages):
        for h in range(group):
            at = i * unit + h * per
            qtmp[at : at + per, :] = qf[i * per : (i + 1) * per, h * HD : (h + 1) * HD]
    qsend[...] = qtmp[...].astype(jnp.bfloat16)
    for k in range(1, n):
        c = to_peer(k, qsend, qg.at[k], qs.at[k], qr.at[k])
        c.start()
        sends.append(c)
    qg[0] = qsend[...]

    for c in c_k + c_v:
        c.wait()
    live = [len_ref[first_own[i]] for i in range(pages)]
    page = [first_own[i] - dp * rows for i in range(pages)]
    place = me * width + iota((unit, width), 1)
    lane = iota((unit, HD), 1)

    def attend(k):
        cols = pl.ds(pl.multiple_of(source(k) * HD, HD), HD)
        packed = []
        for i in range(pages):
            q = qg[k, i * unit : (i + 1) * unit, :]
            valid = place < live[i]
            score = dot(q, kbuf[page[i], :, cols], (((1,), (1,)), ((), ()))) * scale
            score = jnp.where(valid, score, NEG)
            top = jnp.max(score, axis=1, keepdims=True)
            expo = jnp.where(valid, jnp.exp(score - top), 0.0)
            total = jnp.sum(expo, axis=1, keepdims=True)
            acc = dot(expo.astype(jnp.bfloat16), vbuf[page[i], :, cols])
            accs[k, i * unit : (i + 1) * unit, :] = acc.astype(jnp.bfloat16)
            packed.append(jnp.where(lane == 0, top, jnp.where(lane == 1, total, 0.0)))
        mls[k] = jnp.transpose(jnp.concatenate(packed, axis=0))[:8]

    def reply(k):
        dest = {"tensor": source(k)}
        return [
            pltpu.make_async_remote_copy(
                src_ref=accs.at[k], dst_ref=accr.at[k], send_sem=as_.at[k], recv_sem=ar.at[k],
                device_id=dest, device_id_type=pl.DeviceIdType.MESH,
            ),
            pltpu.make_async_remote_copy(
                src_ref=mls.at[k], dst_ref=mlr.at[k], send_sem=ms.at[k], recv_sem=mr.at[k],
                device_id=dest, device_id_type=pl.DeviceIdType.MESH,
            ),
        ]

    def attend_step(k, carry):
        to_peer(k, qsend, qg.at[k], qs.at[k], qr.at[k]).wait_recv()
        attend(k)
        for c in reply(k):
            c.start()
        return carry

    lax.fori_loop(1, n, attend_step, 0)
    attend(0)

    for k in range(1, n):
        to_peer(k, kvg.at[0], kvg.at[source(k) + 1], kvs.at[k], kvr.at[k]).wait_recv()
    kvg[me + 1] = kvg[0]
    per_dev = kv_cols // HD

    def new_head(index):
        return kvg[index // per_dev + 1, :, pl.ds(pl.multiple_of((index % per_dev) * HD, HD), HD)]

    fresh_k = new_head(me)
    fresh_v = new_head(me + KVH)
    q_row = iota((total_rows, R), 0)
    k_row = iota((total_rows, R), 1)
    q_slot = (q_row // unit) * 2 + (q_row % per) // STEPS
    valid = (q_slot == k_row // STEPS) & (k_row % STEPS <= q_row % STEPS)
    score = dot(qsend[...], fresh_k, (((1,), (1,)), ((), ()))) * scale
    score = jnp.where(valid, score, NEG)
    new_top = jnp.max(score, axis=1, keepdims=True)
    expo = jnp.where(valid, jnp.exp(score - new_top), 0.0)
    new_total = jnp.sum(expo, axis=1, keepdims=True)
    new_acc = dot(expo.astype(jnp.bfloat16), fresh_v)
    lane = iota((total_rows, HD), 1)
    new_ml = jnp.transpose(jnp.where(lane == 0, new_top, jnp.where(lane == 1, new_total, 0.0)))

    for k in range(1, n):
        to_peer(k, rw.at[0], rw.at[k], rs.at[k], rr.at[k]).wait_recv()
    sums = jnp.sum(rw[...], axis=0)
    score = sums[1] * lax.rsqrt(sums[0] / (n * feat) + EPS)
    score = jnp.sum(score, axis=1, keepdims=True) / span
    diag = iota((rows, rows), 0) == iota((rows, rows), 1)
    reward_ref[...] = jnp.sum(jnp.where(diag, score, 0.0), axis=0, keepdims=True)

    for k in range(1, n):
        for c in reply(k):
            c.wait_recv()
    tops = [mls[0, 0:1, :]] + [mlr[k, 0:1, :] for k in range(1, n)] + [new_ml[0:1]]
    totals = [mls[0, 1:2, :]] + [mlr[k, 1:2, :] for k in range(1, n)] + [new_ml[1:2]]
    top = functools.reduce(jnp.maximum, tops)
    factors = [jnp.exp(t - top) for t in tops]
    whole = functools.reduce(jnp.add, [f * t for f, t in zip(factors, totals)])
    inverse = 1.0 / whole
    fac[...] = jnp.zeros_like(fac)
    for k in range(n + 1):
        fac[k : k + 1, :] = factors[k] * inverse
    turned = jnp.transpose(fac[...])
    folded = turned[:, n : n + 1] * new_acc + turned[:, 0:1] * accs[0].astype(jnp.float32)
    for k in range(1, n):
        folded = folded + turned[:, k : k + 1] * accr[k].astype(jnp.float32)
    qtmp[...] = folded
    for i in range(pages):
        for h in range(group):
            at = i * unit + h * per
            qf[i * per : (i + 1) * per, h * HD : (h + 1) * HD] = qtmp[at : at + per, :]
    att[...] = qf[...].astype(jnp.bfloat16)

    for c in c_wo:
        c.wait()

    def out_part(k):
        return dot(att[...], wo[:, pl.ds(pl.multiple_of(peer(k) * feat, feat), feat)])

    def out_step(k, carry):
        osend[k] = out_part(k).astype(jnp.bfloat16)
        to_peer(k, osend.at[k], orecv.at[k], os_.at[k], or_.at[k]).start()
        return carry

    lax.fori_loop(1, n, out_step, 0)
    qf[...] = out_part(0)
    summed = qf[...]
    for k in range(1, n):
        to_peer(k, osend.at[k], orecv.at[k], os_.at[k], or_.at[k]).wait_recv()
        summed = summed + orecv[k].astype(jnp.float32)
    fin[dp] = summed.astype(jnp.bfloat16)
    pair_f = to_pair(fin.at[dp], fin.at[dp], fds.at[0], fdr.at[0])
    pair_f.start()
    sends.append(pair_f)

    virtual = jnp.zeros((R, ndp * R), jnp.int32)
    for b in range(ndp):
        for i in range(pages):
            at = b * rows + 2 * i
            virtual = jnp.where(c_i // STEPS == at, first[b][i], virtual)
            virtual = jnp.where(c_i // STEPS == at + 1, second[b][i], virtual)
    place_back = (virtual == dp * rows + r_i % rows) & (c_i % STEPS == r_i // rows)
    place_back = jnp.where(place_back, 1.0, 0.0).astype(jnp.bfloat16)
    pltpu.make_async_remote_copy(
        src_ref=fin.at[other], dst_ref=fin.at[other], send_sem=fds.at[0], recv_sem=fdr.at[0],
        device_id={"dp": other}, device_id_type=pl.DeviceIdType.MESH,
    ).wait_recv()
    out_ref[...] = dot(place_back, fin[...].reshape(ndp * R, feat)).astype(jnp.bfloat16)

    for c in sends:
        c.wait_send()
    for k in range(1, n):
        for c in reply(k):
            c.wait_send()
        to_peer(k, osend.at[k], orecv.at[k], os_.at[k], or_.at[k]).wait_send()


def fused(
    n, ndp,
    reward_hidden, reward_gain, reward_head, decode_inputs, attn_gain, w_query, w_keyval, w_out,
    cache_keys, cache_values, lengths, slot_map,
):
    rows, span, feat = reward_hidden.shape
    width = cache_keys.shape[1]
    R = STEPS * rows
    cols = w_query.shape[1]
    kv_cols = w_keyval.shape[1]
    bf, f32 = jnp.bfloat16, jnp.float32
    total_rows = rows * STEPS * (QH // KVH)
    big = [
        pltpu.VMEM((rows * span, feat), bf),
        pltpu.VMEM(w_query.shape, bf),
        pltpu.VMEM(w_keyval.shape, bf),
        pltpu.VMEM(w_out.shape, bf),
        pltpu.VMEM(cache_keys.shape, bf),
        pltpu.VMEM(cache_values.shape, bf),
    ]
    small = [
        pltpu.VMEM((ndp, R, feat), bf),
        pltpu.VMEM((n, R, feat), bf),
        pltpu.VMEM((R, n * feat), bf),
        pltpu.VMEM((n + 1, R, kv_cols), bf),
        pltpu.VMEM((R, cols), f32),
        pltpu.VMEM((total_rows, HD), f32),
        pltpu.VMEM((total_rows, HD), bf),
        pltpu.VMEM((n, total_rows, HD), bf),
        pltpu.VMEM((n, total_rows, HD), bf),
        pltpu.VMEM((n, total_rows, HD), bf),
        pltpu.VMEM((n, 8, total_rows), f32),
        pltpu.VMEM((n, 8, total_rows), f32),
        pltpu.VMEM((HD, total_rows), f32),
        pltpu.VMEM((R, cols), bf),
        pltpu.VMEM((n, R, feat), bf),
        pltpu.VMEM((n, R, feat), bf),
        pltpu.VMEM((ndp, R, feat), bf),
        pltpu.VMEM((n, 2, rows, span), f32),
    ]
    sem = pltpu.SemaphoreType.DMA
    sems = [sem((17,)), sem((1,)), sem((1,))] + [sem((n,)) for _ in range(14)] + [sem((1,)), sem((1,))]
    vmem, smem, hbm = (pl.BlockSpec(memory_space=m) for m in (pltpu.VMEM, pltpu.SMEM, pl.ANY))
    reward, out = pl.pallas_call(
        functools.partial(kernel, n, ndp, rows, span, width),
        out_shape=(jax.ShapeDtypeStruct((1, rows), f32), jax.ShapeDtypeStruct((R, feat), bf)),
        in_specs=[smem, smem, hbm, vmem, vmem, vmem] + [hbm] * 6,
        out_specs=(vmem, vmem),
        scratch_shapes=big + small + sems,
        compiler_params=pltpu.CompilerParams(
            collective_id=0, has_side_effects=True, vmem_limit_bytes=60 * 2**20
        ),
        name="prune_and_decode",
    )(
        slot_map,
        lengths,
        decode_inputs.reshape(R, feat),
        attn_gain.reshape(1, -1),
        reward_gain.reshape(1, -1),
        reward_head.reshape(1, -1),
        reward_hidden.reshape(rows * span, feat),
        w_query,
        w_keyval,
        w_out,
        cache_keys,
        cache_values,
    )
    return reward.reshape(rows), out.reshape(STEPS, rows, feat)


def device_program(mesh):
    n, ndp = mesh.shape["tensor"], mesh.shape["dp"]
    if n == KVH and ndp == 2:
        return functools.partial(fused, n, ndp)
    return local


def solution(mesh):
    return jax.shard_map(
        device_program(mesh),
        mesh=mesh,
        in_specs=(
            P(("groups", "dp"), None, "tensor"),
            P("tensor"),
            P("tensor"),
            P(None, ("groups", "dp"), "tensor"),
            P(),
            P(None, "tensor"),
            P(None, "tensor"),
            P("tensor", None),
            P(("groups", "dp"), "tensor", None),
            P(("groups", "dp"), "tensor", None),
            P("groups"),
            P("groups"),
        ),
        out_specs=(P(("groups", "dp")), P(None, ("groups", "dp"), "tensor")),
        check_vma=False,
    )
```

```python
import functools

import jax
import jax.numpy as jnp
from jax import lax
from jax.experimental import pallas as pl
from jax.experimental.pallas import tpu as pltpu
from jax.sharding import PartitionSpec as P

D = 8192
QH = 64
KVH = 8
HD = 128
STEPS = 2


EPS = 1e-05
NEG = -1e30


def fold_sources(parts):
    maxima, totals, sums = parts
    top = jnp.max(maxima, axis=0)
    factor = jnp.exp(maxima - top[None])
    return (top, jnp.sum(factor * totals, axis=0), jnp.sum(factor[..., None] * sums, axis=0))


def local(
    reward_hidden,
    reward_gain,
    reward_head,
    decode_inputs,
    attn_gain,
    w_query,
    w_keyval,
    w_out,
    cache_keys,
    cache_values,
    lengths,
    slot_map,
):
    hidden = reward_hidden.astype(jnp.float32)
    squares = jnp.sum(hidden * hidden, axis=-1)
    head_dot = jnp.sum(hidden * (reward_gain * reward_head), axis=-1)
    squares, head_dot = lax.psum((squares, head_dot), "tensor")
    reward = jnp.mean(head_dot * lax.rsqrt(squares / D + EPS), axis=-1)
    rows = cache_keys.shape[0]
    width = cache_keys.shape[1]
    base = lax.axis_index("dp") * rows
    mine = lax.dynamic_slice_in_dim(slot_map, base, rows)
    every_k, every_v = (
        lax.all_gather(cache_keys, "dp", axis=0, tiled=True),
        lax.all_gather(cache_values, "dp", axis=0, tiled=True),
    )
    keys_now = jnp.take(every_k, mine, axis=0)
    values_now = jnp.take(every_v, mine, axis=0)
    live = jnp.take(lengths, mine, axis=0)
    group = QH // KVH
    heads_dev = w_query.shape[1] // HD
    keys4 = keys_now.reshape(rows, width, KVH, HD)
    values4 = values_now.reshape(rows, width, KVH, HD)
    positions = lax.axis_index("tensor") * width + jnp.arange(width)
    valid = (positions[None, :] < live[:, None])[:, None, None, :]
    head_start = lax.axis_index("tensor") * heads_dev
    kv_index = (head_start + jnp.arange(heads_dev)) // group
    scale = HD ** (-0.5)
    new_keys = []
    new_values = []
    outputs = []
    for step in range(STEPS):
        whole = lax.all_gather(decode_inputs[step], "tensor", axis=1, tiled=True).astype(
            jnp.float32
        )
        normed = (
            whole * lax.rsqrt(jnp.mean(whole * whole, axis=-1, keepdims=True) + EPS) * attn_gain
        ).astype(jnp.bfloat16)
        query_part = jnp.dot(normed, w_query, preferred_element_type=jnp.float32).astype(
            jnp.bfloat16
        )
        kv_part = jnp.dot(normed, w_keyval, preferred_element_type=jnp.float32).astype(jnp.bfloat16)
        query_all, keyval = (
            lax.all_gather(query_part, "tensor", axis=1, tiled=True),
            lax.all_gather(kv_part, "tensor", axis=1, tiled=True),
        )
        query = query_all.reshape(rows, KVH, group, HD)
        keyval = keyval.reshape(rows, 2, KVH, HD)
        new_keys.append(keyval[:, 0])
        new_values.append(keyval[:, 1])
        scores = (
            jnp.einsum("rkgd,rwkd->rkgw", query, keys4, preferred_element_type=jnp.float32) * scale
        )
        scores = jnp.where(valid, scores, NEG)
        block_max = jnp.max(scores, axis=-1)
        expo = jnp.where(valid, jnp.exp(scores - block_max[..., None]), 0.0)
        block_total = jnp.sum(expo, axis=-1).reshape(rows, QH)
        block_acc = jnp.einsum(
            "rkgw,rwkd->rkgd",
            expo.astype(jnp.bfloat16),
            values4,
            preferred_element_type=jnp.float32,
        )
        block_acc = block_acc.reshape(rows, QH, HD)
        block_max = block_max.reshape(rows, QH)
        cache_top, cache_total, cache_acc = fold_sources(
            (
                lax.all_to_all(block_max[None], "tensor", split_axis=2, concat_axis=0, tiled=True),
                lax.all_to_all(
                    block_total[None], "tensor", split_axis=2, concat_axis=0, tiled=True
                ),
                lax.all_to_all(block_acc[None], "tensor", split_axis=2, concat_axis=0, tiled=True),
            )
        )
        query_own = query_part.reshape(rows, heads_dev, HD)
        fresh_k = jnp.take(jnp.stack(new_keys, axis=1), kv_index, axis=2)
        fresh_v = jnp.take(jnp.stack(new_values, axis=1), kv_index, axis=2)
        recent = (
            jnp.einsum("rhd,rjhd->rhj", query_own, fresh_k, preferred_element_type=jnp.float32)
            * scale
        )
        recent_max = jnp.max(recent, axis=-1)
        recent_exp = jnp.exp(recent - recent_max[..., None])
        recent_total = jnp.sum(recent_exp, axis=-1)
        recent_acc = jnp.einsum(
            "rhj,rjhd->rhd",
            recent_exp.astype(jnp.bfloat16),
            fresh_v,
            preferred_element_type=jnp.float32,
        )
        top = jnp.maximum(cache_top, recent_max)
        cache_factor = jnp.exp(cache_top - top)
        recent_factor = jnp.exp(recent_max - top)
        total = cache_factor * cache_total + recent_factor * recent_total
        acc = cache_factor[..., None] * cache_acc + recent_factor[..., None] * recent_acc
        attended = (acc / total[..., None]).astype(jnp.bfloat16).reshape(rows, heads_dev * HD)
        partial_out = jnp.dot(attended, w_out, preferred_element_type=jnp.float32)
        summed = lax.psum_scatter(partial_out, "tensor", scatter_dimension=1, tiled=True)
        outputs.append(summed.astype(jnp.bfloat16))
    return (reward, jnp.stack(outputs, axis=0))


def dot(a, b, dims=(((1,), (0,)), ((), ()))):
    return lax.dot_general(a, b, dims, preferred_element_type=jnp.float32)


def iota(shape, dim):
    return lax.broadcasted_iota(jnp.int32, shape, dim)


def kernel(
    n, ndp, rows, span, width,
    map_ref, len_ref, x_hbm, gain_ref, rgain_ref, rhead_ref, rh_hbm, wq_hbm, wkv_hbm, wo_hbm, k_hbm, v_hbm,
    reward_ref, out_ref,
    rh, wq, wkv, wo, kbuf, vbuf,
    xall, xg, normed, kvg, fresh, qf, qtmp, qsend, qg, accs, accr, mls, mlr, fac, att, osend, orecv, fin,
    rw, rwr, rwo,
    loc, xds, xdr, xs, xr, rs, rr, rbs, rbr, kvs, kvr, qs, qr, as_, ar, ms, mr, os_, or_, fds, fdr,
):
    me = lax.axis_index("tensor")
    dp = lax.axis_index("dp")
    other = 1 - dp
    feat = x_hbm.shape[1]
    pages = rows // 2
    per = 2 * STEPS
    R = rows * STEPS
    group = QH // KVH
    unit = group * per
    total_rows = pages * unit
    scale = HD ** (-0.5)

    def peer(k):
        return lax.rem(me + k, n)

    nz = n // 2
    y = lax.rem(me, 2)
    z = me // 2
    mate = me + 1 - 2 * y

    def ahead(k):
        return lax.rem(z + k, nz) * 2 + y

    def ahead_mate(k):
        return lax.rem(z + k, nz) * 2 + 1 - y

    def source(j):
        side = j // nz
        return lax.rem(z + nz - lax.rem(j, nz), nz) * 2 + y + side * (1 - 2 * y)

    copies = []

    def load(src, dst):
        c = pltpu.make_async_copy(src, dst, loc.at[len(copies)])
        c.start()
        copies.append(c)
        return c

    def load_rows(src, dst, parts):
        step = src.shape[0] // parts
        return [load(src.at[pl.ds(i * step, step)], dst.at[pl.ds(i * step, step)]) for i in range(parts)]

    c_x = load(x_hbm, xall.at[dp])
    c_rh = load_rows(rh_hbm, rh, 2)
    c_wkv = load_rows(wkv_hbm, wkv, 2)
    c_wq = load_rows(wq_hbm, wq, 4)
    c_k = load_rows(k_hbm, kbuf, 2)
    c_v = load_rows(v_hbm, vbuf, 2)
    c_wo = load_rows(wo_hbm, wo, 4)

    barrier = pltpu.get_barrier_semaphore()
    for k in range(1, n):
        pl.semaphore_signal(barrier, inc=1, device_id={"tensor": peer(k)}, device_id_type=pl.DeviceIdType.MESH)
    pl.semaphore_signal(barrier, inc=1, device_id={"dp": other}, device_id_type=pl.DeviceIdType.MESH)

    def to_peer(k, src, dst, ssem, rsem):
        return pltpu.make_async_remote_copy(
            src_ref=src, dst_ref=dst, send_sem=ssem, recv_sem=rsem,
            device_id={"tensor": peer(k)}, device_id_type=pl.DeviceIdType.MESH,
        )

    def to_dev(dev, src, dst, ssem, rsem):
        return pltpu.make_async_remote_copy(
            src_ref=src, dst_ref=dst, send_sem=ssem, recv_sem=rsem,
            device_id={"tensor": dev}, device_id_type=pl.DeviceIdType.MESH,
        )

    def to_pair(src, dst, ssem, rsem):
        return pltpu.make_async_remote_copy(
            src_ref=src, dst_ref=dst, send_sem=ssem, recv_sem=rsem,
            device_id={"dp": other}, device_id_type=pl.DeviceIdType.MESH,
        )

    slot = [map_ref[s] for s in range(ndp * rows)]
    first, second = [], []
    for b in range(ndp):
        mine = [jnp.int32(b * rows)] * pages
        count = jnp.int32(0)
        for s in range(b * rows, (b + 1) * rows):
            kept = slot[s] == s
            for i in range(pages):
                mine[i] = jnp.where(kept & (count == i), s, mine[i])
            count = count + jnp.where(kept, 1, 0)
        first.append(mine)
        named = []
        for i in range(pages):
            found = jnp.int32(0)
            for s in range(ndp * rows):
                found = jnp.where((slot[s] == mine[i]) & (mine[i] != s), s, found)
            named.append(found)
        second.append(named)

    def own(lists, i):
        return jnp.where(dp == 0, lists[0][i], lists[1][i])

    first_own = [own(first, i) for i in range(pages)]
    second_own = [own(second, i) for i in range(pages)]

    c_x.wait()
    pl.semaphore_wait(barrier, n)
    pair_x = to_pair(xall.at[dp], xall.at[dp], xds.at[0], xdr.at[0])
    pair_x.start()

    r_i = iota((R, ndp * R), 0)
    c_i = iota((R, ndp * R), 1)
    row_slot = jnp.zeros((R, ndp * R), jnp.int32)
    for i in range(pages):
        row_slot = jnp.where(r_i // STEPS == 2 * i, first_own[i], row_slot)
        row_slot = jnp.where(r_i // STEPS == 2 * i + 1, second_own[i], row_slot)
    col_slot = (c_i // R) * rows + c_i % rows
    pick = (row_slot == col_slot) & (r_i % STEPS == (c_i % R) // rows)
    pick = jnp.where(pick, 1.0, 0.0).astype(jnp.bfloat16)

    pltpu.make_async_remote_copy(
        src_ref=xall.at[other], dst_ref=xall.at[other], send_sem=xds.at[0], recv_sem=xdr.at[0],
        device_id={"dp": other}, device_id_type=pl.DeviceIdType.MESH,
    ).wait_recv()
    chosen = dot(pick, xall[...].reshape(ndp * R, feat))
    xg[me] = chosen.astype(jnp.bfloat16)
    sends = [pair_x]
    for k in range(1, nz):
        c = to_dev(ahead(k), xg.at[me], xg.at[me], xs.at[k], xr.at[k])
        c.start()
        sends.append(c)
    c = to_dev(mate, xg.at[me], xg.at[me], xs.at[nz], xr.at[nz])
    c.start()
    sends.append(c)

    for c in c_rh:
        c.wait()
    weight = rgain_ref[...] * rhead_ref[...]

    def reward_step(r, carry):
        start = pl.multiple_of(r * span, span)
        square = jnp.zeros((span, 128), jnp.float32)
        head = jnp.zeros((span, 128), jnp.float32)
        for b in range(feat // 128):
            h = rh[pl.ds(start, span), b * 128 : (b + 1) * 128].astype(jnp.float32)
            square = square + h * h
            head = head + h * weight[:, b * 128 : (b + 1) * 128]
        rw[r, 0:1, :] = jnp.sum(jnp.transpose(square), axis=0, keepdims=True)
        rw[r, 1:2, :] = jnp.sum(jnp.transpose(head), axis=0, keepdims=True)
        return carry

    lax.fori_loop(0, rows // 2, reward_step, 0)
    for k in range(1, nz):
        s = source(k)
        to_dev(mate, xg.at[s], xg.at[s], xs.at[k], xr.at[k]).wait_recv()
        c = to_dev(mate, xg.at[s], xg.at[s], xs.at[nz + k], xr.at[nz + k])
        c.start()
        sends.append(c)
    lax.fori_loop(rows // 2, rows, reward_step, 0)
    for k in range(1, n):
        c = to_peer(k, rw.at[peer(k)], rwr.at[k], rs.at[k], rr.at[k])
        c.start()
        sends.append(c)
    rwr[0] = rw[me]

    mean = jnp.zeros((R, 1), jnp.float32)
    for j in range(nz, n):
        s = source(j)
        to_dev(mate, xg.at[s], xg.at[s], xs.at[j], xr.at[j]).wait_recv()
    for s in range(n):
        part = xg[s].astype(jnp.float32)
        mean = mean + jnp.sum(part * part, axis=1, keepdims=True)
    factor = lax.rsqrt(mean / (n * feat) + EPS)
    for s in range(n):
        lo, hi = s * feat, (s + 1) * feat
        part = xg[s].astype(jnp.float32)
        normed[:, lo:hi] = (part * factor * gain_ref[:, lo:hi]).astype(jnp.bfloat16)

    for c in c_wkv:
        c.wait()
    keyval = dot(normed[...], wkv[...]).astype(jnp.bfloat16)
    per_dev = wkv.shape[1] // HD
    kind = me * per_dev // KVH
    for p in range(per_dev):
        kvg[p] = keyval[:, p * HD : (p + 1) * HD]
        dest = lax.rem(me * per_dev + p, KVH)

        @pl.when(dest != me)
        def _():
            to_dev(dest, kvg.at[p], fresh.at[kind], kvs.at[p], kvr.at[kind]).start()

        @pl.when(dest == me)
        def _():
            fresh[kind] = kvg[p]

    for c in c_wq:
        c.wait()
    chunk = 256

    def query_step(c, carry):
        cols = pl.ds(pl.multiple_of(c * chunk, chunk), chunk)
        qf[:, cols] = dot(normed[...], wq[:, cols])
        return carry

    lax.fori_loop(0, group * HD // chunk, query_step, 0)
    for i in range(pages):
        for h in range(group):
            at = i * unit + h * per
            qtmp[at : at + per, :] = qf[i * per : (i + 1) * per, h * HD : (h + 1) * HD]
    qsend[...] = qtmp[...].astype(jnp.bfloat16)
    for k in range(1, nz):
        c = to_dev(ahead(k), qsend, qg.at[k], qs.at[k], qr.at[k])
        c.start()
        sends.append(c)
    c = to_dev(mate, qsend, qg.at[nz], qs.at[nz], qr.at[nz])
    c.start()
    sends.append(c)
    qg[0] = qsend[...]

    for c in c_k + c_v:
        c.wait()
    live = [len_ref[first_own[i]] for i in range(pages)]
    page = [first_own[i] - dp * rows for i in range(pages)]
    place = me * width + iota((unit, width), 1)
    lane = iota((unit, HD), 1)

    def attend(k):
        cols = pl.ds(pl.multiple_of(source(k) * HD, HD), HD)
        packed = []
        for i in range(pages):
            q = qg[k, i * unit : (i + 1) * unit, :]
            valid = place < live[i]
            score = dot(q, kbuf[page[i], :, cols], (((1,), (1,)), ((), ()))) * scale
            score = jnp.where(valid, score, NEG)
            top = jnp.max(score, axis=1, keepdims=True)
            expo = jnp.where(valid, jnp.exp(score - top), 0.0)
            total = jnp.sum(expo, axis=1, keepdims=True)
            acc = dot(expo.astype(jnp.bfloat16), vbuf[page[i], :, cols])
            accs[k, i * unit : (i + 1) * unit, :] = acc.astype(jnp.bfloat16)
            packed.append(jnp.where(lane == 0, top, jnp.where(lane == 1, total, 0.0)))
        mls[k] = jnp.transpose(jnp.concatenate(packed, axis=0))[:8]

    def reply(k):
        dest = {"tensor": source(k)}
        return [
            pltpu.make_async_remote_copy(
                src_ref=accs.at[k], dst_ref=accr.at[k], send_sem=as_.at[k], recv_sem=ar.at[k],
                device_id=dest, device_id_type=pl.DeviceIdType.MESH,
            ),
            pltpu.make_async_remote_copy(
                src_ref=mls.at[k], dst_ref=mlr.at[k], send_sem=ms.at[k], recv_sem=mr.at[k],
                device_id=dest, device_id_type=pl.DeviceIdType.MESH,
            ),
        ]

    def arrived(j):
        to_dev(mate, qsend, qg.at[j], qs.at[j], qr.at[j]).wait_recv()

    def hand_on(k):
        return to_dev(mate, qg.at[k], qg.at[nz + k], qs.at[nz + k], qr.at[nz + k])

    def near_step(k, carry):
        arrived(k)
        hand_on(k).start()
        attend(k)
        for c in reply(k):
            c.start()
        return carry

    def far_step(j, carry):
        arrived(j)
        attend(j)
        for c in reply(j):
            c.start()
        return carry

    attend(0)
    lax.fori_loop(1, nz, near_step, 0)
    lax.fori_loop(nz, n, far_step, 0)

    for k in range(1, n):
        to_peer(k, rw.at[0], rwr.at[k], rs.at[k], rr.at[k]).wait_recv()
    sums = jnp.sum(rwr[...], axis=0)
    score = sums[1:2] * lax.rsqrt(sums[0:1] / (n * feat) + EPS)
    rwo[me] = jnp.broadcast_to(jnp.sum(score, axis=1, keepdims=True) / span, rwo.shape[1:])
    for k in range(1, n):
        c = to_peer(k, rwo.at[me], rwo.at[me], rbs.at[k], rbr.at[k])
        c.start()
        sends.append(c)

    for kd in range(2):
        origin = (me + kd * KVH) // per_dev

        @pl.when(origin != me)
        def _():
            to_dev(mate, kvg.at[0], fresh.at[kd], kvs.at[0], kvr.at[kd]).wait_recv()

    fresh_k = fresh[0]
    fresh_v = fresh[1]
    q_row = iota((total_rows, R), 0)
    k_row = iota((total_rows, R), 1)
    q_slot = (q_row // unit) * 2 + (q_row % per) // STEPS
    valid = (q_slot == k_row // STEPS) & (k_row % STEPS <= q_row % STEPS)
    score = dot(qsend[...], fresh_k, (((1,), (1,)), ((), ()))) * scale
    score = jnp.where(valid, score, NEG)
    new_top = jnp.max(score, axis=1, keepdims=True)
    expo = jnp.where(valid, jnp.exp(score - new_top), 0.0)
    new_total = jnp.sum(expo, axis=1, keepdims=True)
    new_acc = dot(expo.astype(jnp.bfloat16), fresh_v)
    lane = iota((total_rows, HD), 1)
    new_ml = jnp.transpose(jnp.where(lane == 0, new_top, jnp.where(lane == 1, new_total, 0.0)))

    for k in range(1, n):
        for c in reply(k):
            c.wait_recv()
    tops = [mls[0, 0:1, :]] + [mlr[k, 0:1, :] for k in range(1, n)] + [new_ml[0:1]]
    totals = [mls[0, 1:2, :]] + [mlr[k, 1:2, :] for k in range(1, n)] + [new_ml[1:2]]
    top = functools.reduce(jnp.maximum, tops)
    factors = [jnp.exp(t - top) for t in tops]
    whole = functools.reduce(jnp.add, [f * t for f, t in zip(factors, totals)])
    inverse = 1.0 / whole
    fac[...] = jnp.zeros_like(fac)
    for k in range(n + 1):
        fac[k : k + 1, :] = factors[k] * inverse
    turned = jnp.transpose(fac[...])
    folded = turned[:, n : n + 1] * new_acc + turned[:, 0:1] * accs[0].astype(jnp.float32)
    for k in range(1, n):
        folded = folded + turned[:, k : k + 1] * accr[k].astype(jnp.float32)
    qtmp[...] = folded
    for i in range(pages):
        for h in range(group):
            at = i * unit + h * per
            qf[i * per : (i + 1) * per, h * HD : (h + 1) * HD] = qtmp[at : at + per, :]
    att[...] = qf[...].astype(jnp.bfloat16)

    for c in c_wo:
        c.wait()

    def out_part(dev):
        return dot(att[...], wo[:, pl.ds(pl.multiple_of(dev * feat, feat), feat)])

    def mate_share(j):
        return to_dev(mate, osend.at[j], orecv.at[j], os_.at[j], or_.at[j])

    def pair_share(k):
        return to_dev(ahead(k), osend.at[k], orecv.at[k], os_.at[k], or_.at[k])

    def mate_step(i, carry):
        k = lax.rem(i, nz)
        osend[nz + k] = out_part(ahead_mate(k)).astype(jnp.bfloat16)
        mate_share(nz + k).start()
        return carry

    def pair_step(k, carry):
        share = out_part(ahead(k))
        mate_share(nz + k).wait_recv()
        osend[k] = (share + orecv[nz + k].astype(jnp.float32)).astype(jnp.bfloat16)
        pair_share(k).start()
        return carry

    lax.fori_loop(1, nz + 1, mate_step, 0)
    lax.fori_loop(1, nz, pair_step, 0)
    qf[...] = out_part(me)
    summed = qf[...]
    mate_share(nz).wait_recv()
    summed = summed + orecv[nz].astype(jnp.float32)
    for k in range(1, nz):
        pair_share(k).wait_recv()
        summed = summed + orecv[k].astype(jnp.float32)
    fin[dp] = summed.astype(jnp.bfloat16)
    pair_f = to_pair(fin.at[dp], fin.at[dp], fds.at[0], fdr.at[0])
    pair_f.start()
    sends.append(pair_f)

    virtual = jnp.zeros((R, ndp * R), jnp.int32)
    for b in range(ndp):
        for i in range(pages):
            at = b * rows + 2 * i
            virtual = jnp.where(c_i // STEPS == at, first[b][i], virtual)
            virtual = jnp.where(c_i // STEPS == at + 1, second[b][i], virtual)
    place_back = (virtual == dp * rows + r_i % rows) & (c_i % STEPS == r_i // rows)
    place_back = jnp.where(place_back, 1.0, 0.0).astype(jnp.bfloat16)
    pltpu.make_async_remote_copy(
        src_ref=fin.at[other], dst_ref=fin.at[other], send_sem=fds.at[0], recv_sem=fdr.at[0],
        device_id={"dp": other}, device_id_type=pl.DeviceIdType.MESH,
    ).wait_recv()
    out_ref[...] = dot(place_back, fin[...].reshape(ndp * R, feat)).astype(jnp.bfloat16)

    result = jnp.zeros((1, rows), jnp.float32)
    for k in range(1, n):
        dev = source(k)
        to_peer(k, rwo.at[me], rwo.at[dev], rbs.at[k], rbr.at[k]).wait_recv()
    for r in range(rows):
        result = jnp.where(iota((1, rows), 1) == r, rwo[r, 0:1, 0:rows], result)
    reward_ref[...] = result

    for c in sends:
        c.wait_send()
    for p in range(per_dev):
        dest = lax.rem(me * per_dev + p, KVH)

        @pl.when(dest != me)
        def _():
            to_dev(dest, kvg.at[p], fresh.at[kind], kvs.at[p], kvr.at[kind]).wait_send()

    for k in range(1, n):
        for c in reply(k):
            c.wait_send()
    for k in range(1, nz):
        hand_on(k).wait_send()
        pair_share(k).wait_send()
    for j in range(nz, n):
        mate_share(j).wait_send()


def write_results(reward_in, out_in, reward_ref, out_ref, sem):
    copies = [
        pltpu.make_async_copy(reward_in, reward_ref, sem.at[0]),
        pltpu.make_async_copy(out_in, out_ref, sem.at[1]),
    ]
    for c in copies:
        c.start()
    for c in copies:
        c.wait()


def fused(
    n, ndp,
    reward_hidden, reward_gain, reward_head, decode_inputs, attn_gain, w_query, w_keyval, w_out,
    cache_keys, cache_values, lengths, slot_map,
):
    rows, span, feat = reward_hidden.shape
    width = cache_keys.shape[1]
    R = STEPS * rows
    cols = w_query.shape[1]
    kv_cols = w_keyval.shape[1]
    bf, f32 = jnp.bfloat16, jnp.float32
    total_rows = rows * STEPS * (QH // KVH)
    big = [
        pltpu.VMEM((rows * span, feat), bf),
        pltpu.VMEM(w_query.shape, bf),
        pltpu.VMEM(w_keyval.shape, bf),
        pltpu.VMEM(w_out.shape, bf),
        pltpu.VMEM(cache_keys.shape, bf),
        pltpu.VMEM(cache_values.shape, bf),
    ]
    small = [
        pltpu.VMEM((ndp, R, feat), bf),
        pltpu.VMEM((n, R, feat), bf),
        pltpu.VMEM((R, n * feat), bf),
        pltpu.VMEM((kv_cols // HD, R, HD), bf),
        pltpu.VMEM((2, R, HD), bf),
        pltpu.VMEM((R, cols), f32),
        pltpu.VMEM((total_rows, HD), f32),
        pltpu.VMEM((total_rows, HD), bf),
        pltpu.VMEM((n, total_rows, HD), bf),
        pltpu.VMEM((n, total_rows, HD), bf),
        pltpu.VMEM((n, total_rows, HD), bf),
        pltpu.VMEM((n, 8, total_rows), f32),
        pltpu.VMEM((n, 8, total_rows), f32),
        pltpu.VMEM((HD, total_rows), f32),
        pltpu.VMEM((R, cols), bf),
        pltpu.VMEM((n, R, feat), bf),
        pltpu.VMEM((n, R, feat), bf),
        pltpu.VMEM((ndp, R, feat), bf),
        pltpu.VMEM((rows, 2, span), f32),
        pltpu.VMEM((n, 2, span), f32),
        pltpu.VMEM((rows, 8, 128), f32),
    ]
    sem = pltpu.SemaphoreType.DMA
    sems = [sem((17,)), sem((1,)), sem((1,))] + [sem((n,)) for _ in range(16)] + [sem((1,)), sem((1,))]
    vmem, smem, hbm = (pl.BlockSpec(memory_space=m) for m in (pltpu.VMEM, pltpu.SMEM, pl.ANY))
    reward, out = pl.pallas_call(
        functools.partial(kernel, n, ndp, rows, span, width),
        out_shape=(jax.ShapeDtypeStruct((1, rows), f32), jax.ShapeDtypeStruct((R, feat), bf)),
        in_specs=[smem, smem, hbm, vmem, vmem, vmem] + [hbm] * 6,
        out_specs=(vmem, vmem),
        scratch_shapes=big + small + sems,
        compiler_params=pltpu.CompilerParams(
            collective_id=0, has_side_effects=True, vmem_limit_bytes=60 * 2**20
        ),
        name="prune_and_decode",
    )(
        slot_map,
        lengths,
        decode_inputs.reshape(R, feat),
        attn_gain.reshape(1, -1),
        reward_gain.reshape(1, -1),
        reward_head.reshape(1, -1),
        reward_hidden.reshape(rows * span, feat),
        w_query,
        w_keyval,
        w_out,
        cache_keys,
        cache_values,
    )
    reward, out = pl.pallas_call(
        write_results,
        out_shape=(jax.ShapeDtypeStruct((1, rows), f32), jax.ShapeDtypeStruct((R, feat), bf)),
        in_specs=[hbm, hbm],
        out_specs=(hbm, hbm),
        scratch_shapes=[sem((2,))],
        name="write_results",
    )(reward, out)
    return reward.reshape(rows), out.reshape(STEPS, rows, feat)


def device_program(mesh):
    n, ndp = mesh.shape["tensor"], mesh.shape["dp"]

    def run(*args):
        if n == KVH and ndp == 2 and args[0].shape[0] == n:
            return fused(n, ndp, *args)
        return local(*args)

    return run


def solution(mesh):
    return jax.shard_map(
        device_program(mesh),
        mesh=mesh,
        in_specs=(
            P(("groups", "dp"), None, "tensor"),
            P("tensor"),
            P("tensor"),
            P(None, ("groups", "dp"), "tensor"),
            P(),
            P(None, "tensor"),
            P(None, "tensor"),
            P("tensor", None),
            P(("groups", "dp"), "tensor", None),
            P(("groups", "dp"), "tensor", None),
            P("groups"),
            P("groups"),
        ),
        out_specs=(P(("groups", "dp")), P(None, ("groups", "dp"), "tensor")),
        check_vma=False,
    )
```

```python
import functools

import jax
import jax.numpy as jnp
from jax import lax
from jax.experimental import pallas as pl
from jax.experimental.pallas import tpu as pltpu
from jax.sharding import PartitionSpec as P

D = 8192
QH = 64
KVH = 8
HD = 128
STEPS = 2


EPS = 1e-05
NEG = -1e30


def fold_sources(parts):
    maxima, totals, sums = parts
    top = jnp.max(maxima, axis=0)
    factor = jnp.exp(maxima - top[None])
    return (top, jnp.sum(factor * totals, axis=0), jnp.sum(factor[..., None] * sums, axis=0))


def local(
    reward_hidden,
    reward_gain,
    reward_head,
    decode_inputs,
    attn_gain,
    w_query,
    w_keyval,
    w_out,
    cache_keys,
    cache_values,
    lengths,
    slot_map,
):
    hidden = reward_hidden.astype(jnp.float32)
    squares = jnp.sum(hidden * hidden, axis=-1)
    head_dot = jnp.sum(hidden * (reward_gain * reward_head), axis=-1)
    squares, head_dot = lax.psum((squares, head_dot), "tensor")
    reward = jnp.mean(head_dot * lax.rsqrt(squares / D + EPS), axis=-1)
    rows = cache_keys.shape[0]
    width = cache_keys.shape[1]
    base = lax.axis_index("dp") * rows
    mine = lax.dynamic_slice_in_dim(slot_map, base, rows)
    every_k, every_v = (
        lax.all_gather(cache_keys, "dp", axis=0, tiled=True),
        lax.all_gather(cache_values, "dp", axis=0, tiled=True),
    )
    keys_now = jnp.take(every_k, mine, axis=0)
    values_now = jnp.take(every_v, mine, axis=0)
    live = jnp.take(lengths, mine, axis=0)
    group = QH // KVH
    heads_dev = w_query.shape[1] // HD
    keys4 = keys_now.reshape(rows, width, KVH, HD)
    values4 = values_now.reshape(rows, width, KVH, HD)
    positions = lax.axis_index("tensor") * width + jnp.arange(width)
    valid = (positions[None, :] < live[:, None])[:, None, None, :]
    head_start = lax.axis_index("tensor") * heads_dev
    kv_index = (head_start + jnp.arange(heads_dev)) // group
    scale = HD ** (-0.5)
    new_keys = []
    new_values = []
    outputs = []
    for step in range(STEPS):
        whole = lax.all_gather(decode_inputs[step], "tensor", axis=1, tiled=True).astype(
            jnp.float32
        )
        normed = (
            whole * lax.rsqrt(jnp.mean(whole * whole, axis=-1, keepdims=True) + EPS) * attn_gain
        ).astype(jnp.bfloat16)
        query_part = jnp.dot(normed, w_query, preferred_element_type=jnp.float32).astype(
            jnp.bfloat16
        )
        kv_part = jnp.dot(normed, w_keyval, preferred_element_type=jnp.float32).astype(jnp.bfloat16)
        query_all, keyval = (
            lax.all_gather(query_part, "tensor", axis=1, tiled=True),
            lax.all_gather(kv_part, "tensor", axis=1, tiled=True),
        )
        query = query_all.reshape(rows, KVH, group, HD)
        keyval = keyval.reshape(rows, 2, KVH, HD)
        new_keys.append(keyval[:, 0])
        new_values.append(keyval[:, 1])
        scores = (
            jnp.einsum("rkgd,rwkd->rkgw", query, keys4, preferred_element_type=jnp.float32) * scale
        )
        scores = jnp.where(valid, scores, NEG)
        block_max = jnp.max(scores, axis=-1)
        expo = jnp.where(valid, jnp.exp(scores - block_max[..., None]), 0.0)
        block_total = jnp.sum(expo, axis=-1).reshape(rows, QH)
        block_acc = jnp.einsum(
            "rkgw,rwkd->rkgd",
            expo.astype(jnp.bfloat16),
            values4,
            preferred_element_type=jnp.float32,
        )
        block_acc = block_acc.reshape(rows, QH, HD)
        block_max = block_max.reshape(rows, QH)
        cache_top, cache_total, cache_acc = fold_sources(
            (
                lax.all_to_all(block_max[None], "tensor", split_axis=2, concat_axis=0, tiled=True),
                lax.all_to_all(
                    block_total[None], "tensor", split_axis=2, concat_axis=0, tiled=True
                ),
                lax.all_to_all(block_acc[None], "tensor", split_axis=2, concat_axis=0, tiled=True),
            )
        )
        query_own = query_part.reshape(rows, heads_dev, HD)
        fresh_k = jnp.take(jnp.stack(new_keys, axis=1), kv_index, axis=2)
        fresh_v = jnp.take(jnp.stack(new_values, axis=1), kv_index, axis=2)
        recent = (
            jnp.einsum("rhd,rjhd->rhj", query_own, fresh_k, preferred_element_type=jnp.float32)
            * scale
        )
        recent_max = jnp.max(recent, axis=-1)
        recent_exp = jnp.exp(recent - recent_max[..., None])
        recent_total = jnp.sum(recent_exp, axis=-1)
        recent_acc = jnp.einsum(
            "rhj,rjhd->rhd",
            recent_exp.astype(jnp.bfloat16),
            fresh_v,
            preferred_element_type=jnp.float32,
        )
        top = jnp.maximum(cache_top, recent_max)
        cache_factor = jnp.exp(cache_top - top)
        recent_factor = jnp.exp(recent_max - top)
        total = cache_factor * cache_total + recent_factor * recent_total
        acc = cache_factor[..., None] * cache_acc + recent_factor[..., None] * recent_acc
        attended = (acc / total[..., None]).astype(jnp.bfloat16).reshape(rows, heads_dev * HD)
        partial_out = jnp.dot(attended, w_out, preferred_element_type=jnp.float32)
        summed = lax.psum_scatter(partial_out, "tensor", scatter_dimension=1, tiled=True)
        outputs.append(summed.astype(jnp.bfloat16))
    return (reward, jnp.stack(outputs, axis=0))


def dot(a, b, dims=(((1,), (0,)), ((), ()))):
    return lax.dot_general(a, b, dims, preferred_element_type=jnp.float32)


def iota(shape, dim):
    return lax.broadcasted_iota(jnp.int32, shape, dim)


def kernel(
    n, ndp, rows, span, width,
    map_ref, len_ref, x_hbm, gain_ref, rgain_ref, rhead_ref, rh_hbm, wq_hbm, wkv_hbm, wo_hbm, k_hbm, v_hbm,
    reward_ref, out_ref,
    rh, wq, wkv, wo, kbuf, vbuf,
    xg, normed, kvg, fresh, qf, qtmp, hq, qhalf, attf, qsend, qg, accs, accr, mls, mlr, fac, att, osend, orecv, hfin, fin,
    rw, rwr, rwo,
    loc, xps, xpr, xs, xr, rs, rr, rbs, rbr, kvs, kvr, qs, qr, as_, ar, ms, mr, os_, or_, fds, fdr, hqs, hqr, ats, atr,
):
    me = lax.axis_index("tensor")
    dp = lax.axis_index("dp")
    other = 1 - dp
    feat = x_hbm.shape[1]
    pages = rows // 2
    per = 2 * STEPS
    R = rows * STEPS
    group = QH // KVH
    unit = group * per
    total_rows = pages * unit
    scale = HD ** (-0.5)

    def peer(k):
        return lax.rem(me + k, n)

    nz = n // 2
    y = lax.rem(me, 2)
    z = me // 2
    mate = me + 1 - 2 * y

    def ahead(k):
        return lax.rem(z + k, nz) * 2 + y

    def ahead_mate(k):
        return lax.rem(z + k, nz) * 2 + 1 - y

    def source(j):
        side = j // nz
        return lax.rem(z + nz - lax.rem(j, nz), nz) * 2 + y + side * (1 - 2 * y)

    copies = []

    def load(src, dst):
        c = pltpu.make_async_copy(src, dst, loc.at[len(copies)])
        c.start()
        copies.append(c)
        return c

    def load_rows(src, dst, parts):
        step = src.shape[0] // parts
        return [load(src.at[pl.ds(i * step, step)], dst.at[pl.ds(i * step, step)]) for i in range(parts)]

    c_x = load(x_hbm, xg.at[dp, me])
    c_rh = load_rows(rh_hbm, rh, 2)
    c_wkv = load_rows(wkv_hbm, wkv, 2)
    half = wq.shape[1]
    c_wq = load_rows(wq_hbm.at[:, pl.ds(pl.multiple_of(dp * half, half), half)], wq, 4)
    c_k = load_rows(k_hbm, kbuf, 2)
    c_v = load_rows(v_hbm, vbuf, 2)
    out_half = feat // ndp
    c_wo = [
        load(wo_hbm.at[:, pl.ds(pl.multiple_of(s * feat + dp * out_half, out_half), out_half)], wo.at[s])
        for s in range(n)
    ]

    barrier = pltpu.get_barrier_semaphore()
    for k in range(1, n):
        pl.semaphore_signal(barrier, inc=1, device_id={"tensor": peer(k)}, device_id_type=pl.DeviceIdType.MESH)
    pl.semaphore_signal(barrier, inc=1, device_id={"dp": other}, device_id_type=pl.DeviceIdType.MESH)

    def to_peer(k, src, dst, ssem, rsem):
        return pltpu.make_async_remote_copy(
            src_ref=src, dst_ref=dst, send_sem=ssem, recv_sem=rsem,
            device_id={"tensor": peer(k)}, device_id_type=pl.DeviceIdType.MESH,
        )

    def to_dev(dev, src, dst, ssem, rsem):
        return pltpu.make_async_remote_copy(
            src_ref=src, dst_ref=dst, send_sem=ssem, recv_sem=rsem,
            device_id={"tensor": dev}, device_id_type=pl.DeviceIdType.MESH,
        )

    def to_pair(src, dst, ssem, rsem):
        return pltpu.make_async_remote_copy(
            src_ref=src, dst_ref=dst, send_sem=ssem, recv_sem=rsem,
            device_id={"dp": other}, device_id_type=pl.DeviceIdType.MESH,
        )

    slot = [map_ref[s] for s in range(ndp * rows)]
    first, second = [], []
    for b in range(ndp):
        mine = [jnp.int32(b * rows)] * pages
        count = jnp.int32(0)
        for s in range(b * rows, (b + 1) * rows):
            kept = slot[s] == s
            for i in range(pages):
                mine[i] = jnp.where(kept & (count == i), s, mine[i])
            count = count + jnp.where(kept, 1, 0)
        first.append(mine)
        named = []
        for i in range(pages):
            found = jnp.int32(0)
            for s in range(ndp * rows):
                found = jnp.where((slot[s] == mine[i]) & (mine[i] != s), s, found)
            named.append(found)
        second.append(named)

    def own(lists, i):
        return jnp.where(dp == 0, lists[0][i], lists[1][i])

    first_own = [own(first, i) for i in range(pages)]
    second_own = [own(second, i) for i in range(pages)]

    c_x.wait()
    pl.semaphore_wait(barrier, n)
    sends = []

    def pass_on(s, j):
        return to_pair(xg.at[dp, s], xg.at[dp, s], xps.at[j], xpr.at[j])

    def hand_x(dev, s, j):
        return to_dev(dev, xg.at[dp, s], xg.at[dp, s], xs.at[j], xr.at[j])

    for c in [hand_x(ahead(k), me, k) for k in range(1, nz)] + [hand_x(mate, me, nz), pass_on(me, 0)]:
        c.start()
        sends.append(c)

    r_i = iota((R, ndp * R), 0)
    c_i = iota((R, ndp * R), 1)
    row_slot = jnp.zeros((R, ndp * R), jnp.int32)
    for i in range(pages):
        row_slot = jnp.where(r_i // STEPS == 2 * i, first_own[i], row_slot)
        row_slot = jnp.where(r_i // STEPS == 2 * i + 1, second_own[i], row_slot)
    col_slot = (c_i // R) * rows + c_i % rows
    pick = (row_slot == col_slot) & (r_i % STEPS == (c_i % R) // rows)
    pick = jnp.where(pick, 1.0, 0.0).astype(jnp.bfloat16)

    r_i = iota((ndp * R, ndp * R), 0)
    c_i = iota((ndp * R, ndp * R), 1)
    by_row = jnp.zeros(r_i.shape, jnp.int32)
    by_col = jnp.zeros(r_i.shape, jnp.int32)
    for b in range(ndp):
        for i in range(pages):
            at = b * rows + 2 * i
            by_row = jnp.where(r_i // STEPS == at, first[b][i], by_row)
            by_row = jnp.where(r_i // STEPS == at + 1, second[b][i], by_row)
            by_col = jnp.where(c_i // STEPS == at, first[b][i], by_col)
            by_col = jnp.where(c_i // STEPS == at + 1, second[b][i], by_col)
    pick_all = (by_row == (c_i // R) * rows + c_i % rows) & (r_i % STEPS == (c_i % R) // rows)
    pick_all = jnp.where(pick_all, 1.0, 0.0).astype(jnp.bfloat16)
    put_all = (by_col == (r_i // R) * rows + r_i % rows) & (c_i % STEPS == (r_i % R) // rows)
    put_all = jnp.where(put_all, 1.0, 0.0).astype(jnp.bfloat16)

    for c in c_rh:
        c.wait()
    weight = rgain_ref[...] * rhead_ref[...]

    def reward_step(r, carry):
        start = pl.multiple_of(r * span, span)
        square = jnp.zeros((span, 128), jnp.float32)
        head = jnp.zeros((span, 128), jnp.float32)
        for b in range(feat // 128):
            h = rh[pl.ds(start, span), b * 128 : (b + 1) * 128].astype(jnp.float32)
            square = square + h * h
            head = head + h * weight[:, b * 128 : (b + 1) * 128]
        rw[r, 0:1, :] = jnp.sum(jnp.transpose(square), axis=0, keepdims=True)
        rw[r, 1:2, :] = jnp.sum(jnp.transpose(head), axis=0, keepdims=True)
        return carry

    lax.fori_loop(0, rows // 2, reward_step, 0)
    for k in range(1, nz):
        s = source(k)
        hand_x(mate, s, k).wait_recv()
        for c in (hand_x(mate, s, nz + k), pass_on(s, k)):
            c.start()
            sends.append(c)
    lax.fori_loop(rows // 2, rows, reward_step, 0)
    for k in range(1, n):
        c = to_peer(k, rw.at[peer(k)], rwr.at[k], rs.at[k], rr.at[k])
        c.start()
        sends.append(c)
    rwr[0] = rw[me]

    for j in range(nz, n):
        s = source(j)
        hand_x(mate, s, j).wait_recv()
        c = pass_on(s, j)
        c.start()
        sends.append(c)
    for j in range(n):
        s = source(j)
        to_pair(xg.at[other, s], xg.at[other, s], xps.at[j], xpr.at[j]).wait_recv()
    mean = jnp.zeros((ndp * R, 1), jnp.float32)
    for s in range(n):
        part = xg[:, s].reshape(ndp * R, feat).astype(jnp.float32)
        mean = mean + jnp.sum(part * part, axis=1, keepdims=True)
    factor = lax.rsqrt(mean / (n * feat) + EPS)
    for s in range(n):
        lo, hi = s * feat, (s + 1) * feat
        part = xg[:, s].reshape(ndp * R, feat).astype(jnp.float32)
        normed[:, lo:hi] = (part * factor * gain_ref[:, lo:hi]).astype(jnp.bfloat16)

    for c in c_wkv:
        c.wait()
    keyval = dot(normed[...], wkv[...]).astype(jnp.bfloat16)
    keyval = dot(pick, keyval).astype(jnp.bfloat16)
    per_dev = wkv.shape[1] // HD
    kind = me * per_dev // KVH
    for p in range(per_dev):
        kvg[p] = keyval[:, p * HD : (p + 1) * HD]
        dest = lax.rem(me * per_dev + p, KVH)

        @pl.when(dest != me)
        def _():
            to_dev(dest, kvg.at[p], fresh.at[kind], kvs.at[p], kvr.at[kind]).start()

        @pl.when(dest == me)
        def _():
            fresh[kind] = kvg[p]

    for c in c_wq:
        c.wait()
    chunk = 256

    def query_step(c, carry):
        cols = pl.ds(pl.multiple_of(c * chunk, chunk), chunk)
        qf[:, cols] = dot(normed[...], wq[:, cols])
        return carry

    lax.fori_loop(0, half // chunk, query_step, 0)
    qf[...] = dot(pick_all, qf[...].astype(jnp.bfloat16))
    heads = half // HD
    small = heads * per
    for b in range(ndp):
        for i in range(pages):
            for h in range(heads):
                at = i * small + h * per
                row = b * R + i * per
                qtmp[at : at + per, :] = qf[row : row + per, h * HD : (h + 1) * HD]
        hq[b] = qtmp[0 : pages * small, :].astype(jnp.bfloat16)
    swap_q = to_pair(hq.at[other], qhalf.at[dp], hqs.at[0], hqr.at[0])
    swap_q.start()
    sends.append(swap_q)
    qhalf[dp] = hq[dp]
    to_pair(hq.at[other], qhalf.at[other], hqs.at[0], hqr.at[0]).wait_recv()
    for i in range(pages):
        for b in range(ndp):
            at = i * unit + b * small
            qsend[at : at + small, :] = qhalf[b, i * small : (i + 1) * small, :]
    for k in range(1, nz):
        c = to_dev(ahead(k), qsend, qg.at[k], qs.at[k], qr.at[k])
        c.start()
        sends.append(c)
    c = to_dev(mate, qsend, qg.at[nz], qs.at[nz], qr.at[nz])
    c.start()
    sends.append(c)
    qg[0] = qsend[...]

    for c in c_k + c_v:
        c.wait()
    live = [len_ref[first_own[i]] for i in range(pages)]
    page = [first_own[i] - dp * rows for i in range(pages)]
    place = me * width + iota((unit, width), 1)
    lane = iota((unit, HD), 1)

    def attend(k):
        cols = pl.ds(pl.multiple_of(source(k) * HD, HD), HD)
        packed = []
        for i in range(pages):
            q = qg[k, i * unit : (i + 1) * unit, :]
            valid = place < live[i]
            score = dot(q, kbuf[page[i], :, cols], (((1,), (1,)), ((), ()))) * scale
            score = jnp.where(valid, score, NEG)
            top = jnp.max(score, axis=1, keepdims=True)
            expo = jnp.where(valid, jnp.exp(score - top), 0.0)
            total = jnp.sum(expo, axis=1, keepdims=True)
            acc = dot(expo.astype(jnp.bfloat16), vbuf[page[i], :, cols])
            accs[k, i * unit : (i + 1) * unit, :] = acc.astype(jnp.bfloat16)
            packed.append(jnp.where(lane == 0, top, jnp.where(lane == 1, total, 0.0)))
        mls[k] = jnp.transpose(jnp.concatenate(packed, axis=0))[:8]

    def reply(k):
        dest = {"tensor": source(k)}
        return [
            pltpu.make_async_remote_copy(
                src_ref=accs.at[k], dst_ref=accr.at[k], send_sem=as_.at[k], recv_sem=ar.at[k],
                device_id=dest, device_id_type=pl.DeviceIdType.MESH,
            ),
            pltpu.make_async_remote_copy(
                src_ref=mls.at[k], dst_ref=mlr.at[k], send_sem=ms.at[k], recv_sem=mr.at[k],
                device_id=dest, device_id_type=pl.DeviceIdType.MESH,
            ),
        ]

    def arrived(j):
        to_dev(mate, qsend, qg.at[j], qs.at[j], qr.at[j]).wait_recv()

    def hand_on(k):
        return to_dev(mate, qg.at[k], qg.at[nz + k], qs.at[nz + k], qr.at[nz + k])

    def near_step(k, carry):
        arrived(k)
        hand_on(k).start()
        attend(k)
        for c in reply(k):
            c.start()
        return carry

    def far_step(j, carry):
        arrived(j)
        attend(j)
        for c in reply(j):
            c.start()
        return carry

    attend(0)
    lax.fori_loop(1, nz, near_step, 0)
    lax.fori_loop(nz, n, far_step, 0)

    for k in range(1, n):
        to_peer(k, rw.at[0], rwr.at[k], rs.at[k], rr.at[k]).wait_recv()
    sums = jnp.sum(rwr[...], axis=0)
    score = sums[1:2] * lax.rsqrt(sums[0:1] / (n * feat) + EPS)
    rwo[me] = jnp.broadcast_to(jnp.sum(score, axis=1, keepdims=True) / span, rwo.shape[1:])
    for k in range(1, n):
        c = to_peer(k, rwo.at[me], rwo.at[me], rbs.at[k], rbr.at[k])
        c.start()
        sends.append(c)

    for kd in range(2):
        origin = (me + kd * KVH) // per_dev

        @pl.when(origin != me)
        def _():
            to_dev(mate, kvg.at[0], fresh.at[kd], kvs.at[0], kvr.at[kd]).wait_recv()

    fresh_k = fresh[0]
    fresh_v = fresh[1]
    q_row = iota((total_rows, R), 0)
    k_row = iota((total_rows, R), 1)
    q_slot = (q_row // unit) * 2 + (q_row % per) // STEPS
    valid = (q_slot == k_row // STEPS) & (k_row % STEPS <= q_row % STEPS)
    score = dot(qsend[...], fresh_k, (((1,), (1,)), ((), ()))) * scale
    score = jnp.where(valid, score, NEG)
    new_top = jnp.max(score, axis=1, keepdims=True)
    expo = jnp.where(valid, jnp.exp(score - new_top), 0.0)
    new_total = jnp.sum(expo, axis=1, keepdims=True)
    new_acc = dot(expo.astype(jnp.bfloat16), fresh_v)
    lane = iota((total_rows, HD), 1)
    new_ml = jnp.transpose(jnp.where(lane == 0, new_top, jnp.where(lane == 1, new_total, 0.0)))

    for k in range(1, n):
        for c in reply(k):
            c.wait_recv()
    tops = [mls[0, 0:1, :]] + [mlr[k, 0:1, :] for k in range(1, n)] + [new_ml[0:1]]
    totals = [mls[0, 1:2, :]] + [mlr[k, 1:2, :] for k in range(1, n)] + [new_ml[1:2]]
    top = functools.reduce(jnp.maximum, tops)
    factors = [jnp.exp(t - top) for t in tops]
    whole = functools.reduce(jnp.add, [f * t for f, t in zip(factors, totals)])
    inverse = 1.0 / whole
    fac[...] = jnp.zeros_like(fac)
    for k in range(n + 1):
        fac[k : k + 1, :] = factors[k] * inverse
    turned = jnp.transpose(fac[...])
    folded = turned[:, n : n + 1] * new_acc + turned[:, 0:1] * accs[0].astype(jnp.float32)
    for k in range(1, n):
        folded = folded + turned[:, k : k + 1] * accr[k].astype(jnp.float32)
    qtmp[...] = folded
    for i in range(pages):
        for h in range(group):
            at = i * unit + h * per
            attf[i * per : (i + 1) * per, h * HD : (h + 1) * HD] = qtmp[at : at + per, :]
    att[dp] = attf[...].astype(jnp.bfloat16)
    swap_a = to_pair(att.at[dp], att.at[dp], ats.at[0], atr.at[0])
    swap_a.start()
    sends.append(swap_a)
    to_pair(att.at[other], att.at[other], ats.at[0], atr.at[0]).wait_recv()

    for c in c_wo:
        c.wait()

    def out_part(dev):
        return dot(att[...].reshape(ndp * R, att.shape[2]), wo[dev])

    def mate_share(j):
        return to_dev(mate, osend.at[j], orecv.at[j], os_.at[j], or_.at[j])

    def pair_share(k):
        return to_dev(ahead(k), osend.at[k], orecv.at[k], os_.at[k], or_.at[k])

    def mate_step(i, carry):
        k = lax.rem(i, nz)
        osend[nz + k] = out_part(ahead_mate(k)).astype(jnp.bfloat16)
        mate_share(nz + k).start()
        return carry

    def pair_step(k, carry):
        share = out_part(ahead(k))
        mate_share(nz + k).wait_recv()
        osend[k] = (share + orecv[nz + k].astype(jnp.float32)).astype(jnp.bfloat16)
        pair_share(k).start()
        return carry

    lax.fori_loop(1, nz + 1, mate_step, 0)
    lax.fori_loop(1, nz, pair_step, 0)
    summed = out_part(me)
    mate_share(nz).wait_recv()
    summed = summed + orecv[nz].astype(jnp.float32)
    for k in range(1, nz):
        pair_share(k).wait_recv()
        summed = summed + orecv[k].astype(jnp.float32)
    placed = dot(put_all, summed.astype(jnp.bfloat16)).astype(jnp.bfloat16)
    hfin[...] = placed.reshape(ndp, R, out_half)
    pair_f = to_pair(hfin.at[other], fin.at[dp], fds.at[0], fdr.at[0])
    pair_f.start()
    sends.append(pair_f)
    fin[dp] = hfin[dp]
    to_pair(hfin.at[other], fin.at[other], fds.at[0], fdr.at[0]).wait_recv()
    for b in range(ndp):
        out_ref[:, b * out_half : (b + 1) * out_half] = fin[b]

    result = jnp.zeros((1, rows), jnp.float32)
    for k in range(1, n):
        dev = source(k)
        to_peer(k, rwo.at[me], rwo.at[dev], rbs.at[k], rbr.at[k]).wait_recv()
    for r in range(rows):
        result = jnp.where(iota((1, rows), 1) == r, rwo[r, 0:1, 0:rows], result)
    reward_ref[...] = result

    for c in sends:
        c.wait_send()
    for p in range(per_dev):
        dest = lax.rem(me * per_dev + p, KVH)

        @pl.when(dest != me)
        def _():
            to_dev(dest, kvg.at[p], fresh.at[kind], kvs.at[p], kvr.at[kind]).wait_send()

    for k in range(1, n):
        for c in reply(k):
            c.wait_send()
    for k in range(1, nz):
        hand_on(k).wait_send()
        pair_share(k).wait_send()
    for j in range(nz, n):
        mate_share(j).wait_send()


def write_results(reward_in, out_in, reward_ref, out_ref, sem):
    copies = [
        pltpu.make_async_copy(reward_in, reward_ref, sem.at[0]),
        pltpu.make_async_copy(out_in, out_ref, sem.at[1]),
    ]
    for c in copies:
        c.start()
    for c in copies:
        c.wait()


def fused(
    n, ndp,
    reward_hidden, reward_gain, reward_head, decode_inputs, attn_gain, w_query, w_keyval, w_out,
    cache_keys, cache_values, lengths, slot_map,
):
    rows, span, feat = reward_hidden.shape
    width = cache_keys.shape[1]
    R = STEPS * rows
    cols = w_query.shape[1]
    kv_cols = w_keyval.shape[1]
    bf, f32 = jnp.bfloat16, jnp.float32
    total_rows = rows * STEPS * (QH // KVH)
    big = [
        pltpu.VMEM((rows * span, feat), bf),
        pltpu.VMEM((n * feat, cols // ndp), bf),
        pltpu.VMEM(w_keyval.shape, bf),
        pltpu.VMEM((n, w_out.shape[0], feat // ndp), bf),
        pltpu.VMEM(cache_keys.shape, bf),
        pltpu.VMEM(cache_values.shape, bf),
    ]
    small = [
        pltpu.VMEM((ndp, n, R, feat), bf),
        pltpu.VMEM((ndp * R, n * feat), bf),
        pltpu.VMEM((kv_cols // HD, R, HD), bf),
        pltpu.VMEM((2, R, HD), bf),
        pltpu.VMEM((ndp * R, cols // ndp), f32),
        pltpu.VMEM((total_rows, HD), f32),
        pltpu.VMEM((ndp, total_rows // ndp, HD), bf),
        pltpu.VMEM((ndp, total_rows // ndp, HD), bf),
        pltpu.VMEM((R, cols), f32),
        pltpu.VMEM((total_rows, HD), bf),
        pltpu.VMEM((n, total_rows, HD), bf),
        pltpu.VMEM((n, total_rows, HD), bf),
        pltpu.VMEM((n, total_rows, HD), bf),
        pltpu.VMEM((n, 8, total_rows), f32),
        pltpu.VMEM((n, 8, total_rows), f32),
        pltpu.VMEM((HD, total_rows), f32),
        pltpu.VMEM((ndp, R, cols), bf),
        pltpu.VMEM((n, ndp * R, feat // ndp), bf),
        pltpu.VMEM((n, ndp * R, feat // ndp), bf),
        pltpu.VMEM((ndp, R, feat // ndp), bf),
        pltpu.VMEM((ndp, R, feat // ndp), bf),
        pltpu.VMEM((rows, 2, span), f32),
        pltpu.VMEM((n, 2, span), f32),
        pltpu.VMEM((rows, 8, 128), f32),
    ]
    sem = pltpu.SemaphoreType.DMA
    sems = [sem((13 + n,))] + [sem((n,)) for _ in range(18)] + [sem((1,)) for _ in range(6)]
    vmem, smem, hbm = (pl.BlockSpec(memory_space=m) for m in (pltpu.VMEM, pltpu.SMEM, pl.ANY))
    reward, out = pl.pallas_call(
        functools.partial(kernel, n, ndp, rows, span, width),
        out_shape=(jax.ShapeDtypeStruct((1, rows), f32), jax.ShapeDtypeStruct((R, feat), bf)),
        in_specs=[smem, smem, hbm, vmem, vmem, vmem] + [hbm] * 6,
        out_specs=(vmem, vmem),
        scratch_shapes=big + small + sems,
        compiler_params=pltpu.CompilerParams(
            collective_id=0, has_side_effects=True, vmem_limit_bytes=60 * 2**20
        ),
        name="prune_and_decode",
    )(
        slot_map,
        lengths,
        decode_inputs.reshape(R, feat),
        attn_gain.reshape(1, -1),
        reward_gain.reshape(1, -1),
        reward_head.reshape(1, -1),
        reward_hidden.reshape(rows * span, feat),
        w_query,
        w_keyval,
        w_out,
        cache_keys,
        cache_values,
    )
    reward, out = pl.pallas_call(
        write_results,
        out_shape=(jax.ShapeDtypeStruct((1, rows), f32), jax.ShapeDtypeStruct((R, feat), bf)),
        in_specs=[hbm, hbm],
        out_specs=(hbm, hbm),
        scratch_shapes=[sem((2,))],
        name="write_results",
    )(reward, out)
    return reward.reshape(rows), out.reshape(STEPS, rows, feat)


def device_program(mesh):
    n, ndp = mesh.shape["tensor"], mesh.shape["dp"]

    def run(*args):
        if n == KVH and ndp == 2 and args[0].shape[0] == n:
            return fused(n, ndp, *args)
        return local(*args)

    return run


def solution(mesh):
    return jax.shard_map(
        device_program(mesh),
        mesh=mesh,
        in_specs=(
            P(("groups", "dp"), None, "tensor"),
            P("tensor"),
            P("tensor"),
            P(None, ("groups", "dp"), "tensor"),
            P(),
            P(None, "tensor"),
            P(None, "tensor"),
            P("tensor", None),
            P(("groups", "dp"), "tensor", None),
            P(("groups", "dp"), "tensor", None),
            P("groups"),
            P("groups"),
        ),
        out_specs=(P(("groups", "dp")), P(None, ("groups", "dp"), "tensor")),
        check_vma=False,
    )
```

```python
import functools

import jax
import jax.numpy as jnp
from jax import lax
from jax.experimental import pallas as pl
from jax.experimental.pallas import tpu as pltpu
from jax.sharding import PartitionSpec as P

D = 8192
QH = 64
KVH = 8
HD = 128
STEPS = 2


EPS = 1e-05
NEG = -1e30


def fold_sources(parts):
    maxima, totals, sums = parts
    top = jnp.max(maxima, axis=0)
    factor = jnp.exp(maxima - top[None])
    return (top, jnp.sum(factor * totals, axis=0), jnp.sum(factor[..., None] * sums, axis=0))


def local(
    reward_hidden,
    reward_gain,
    reward_head,
    decode_inputs,
    attn_gain,
    w_query,
    w_keyval,
    w_out,
    cache_keys,
    cache_values,
    lengths,
    slot_map,
):
    hidden = reward_hidden.astype(jnp.float32)
    squares = jnp.sum(hidden * hidden, axis=-1)
    head_dot = jnp.sum(hidden * (reward_gain * reward_head), axis=-1)
    squares, head_dot = lax.psum((squares, head_dot), "tensor")
    reward = jnp.mean(head_dot * lax.rsqrt(squares / D + EPS), axis=-1)
    rows = cache_keys.shape[0]
    width = cache_keys.shape[1]
    base = lax.axis_index("dp") * rows
    mine = lax.dynamic_slice_in_dim(slot_map, base, rows)
    every_k, every_v = (
        lax.all_gather(cache_keys, "dp", axis=0, tiled=True),
        lax.all_gather(cache_values, "dp", axis=0, tiled=True),
    )
    keys_now = jnp.take(every_k, mine, axis=0)
    values_now = jnp.take(every_v, mine, axis=0)
    live = jnp.take(lengths, mine, axis=0)
    group = QH // KVH
    heads_dev = w_query.shape[1] // HD
    keys4 = keys_now.reshape(rows, width, KVH, HD)
    values4 = values_now.reshape(rows, width, KVH, HD)
    positions = lax.axis_index("tensor") * width + jnp.arange(width)
    valid = (positions[None, :] < live[:, None])[:, None, None, :]
    head_start = lax.axis_index("tensor") * heads_dev
    kv_index = (head_start + jnp.arange(heads_dev)) // group
    scale = HD ** (-0.5)
    new_keys = []
    new_values = []
    outputs = []
    for step in range(STEPS):
        whole = lax.all_gather(decode_inputs[step], "tensor", axis=1, tiled=True).astype(
            jnp.float32
        )
        normed = (
            whole * lax.rsqrt(jnp.mean(whole * whole, axis=-1, keepdims=True) + EPS) * attn_gain
        ).astype(jnp.bfloat16)
        query_part = jnp.dot(normed, w_query, preferred_element_type=jnp.float32).astype(
            jnp.bfloat16
        )
        kv_part = jnp.dot(normed, w_keyval, preferred_element_type=jnp.float32).astype(jnp.bfloat16)
        query_all, keyval = (
            lax.all_gather(query_part, "tensor", axis=1, tiled=True),
            lax.all_gather(kv_part, "tensor", axis=1, tiled=True),
        )
        query = query_all.reshape(rows, KVH, group, HD)
        keyval = keyval.reshape(rows, 2, KVH, HD)
        new_keys.append(keyval[:, 0])
        new_values.append(keyval[:, 1])
        scores = (
            jnp.einsum("rkgd,rwkd->rkgw", query, keys4, preferred_element_type=jnp.float32) * scale
        )
        scores = jnp.where(valid, scores, NEG)
        block_max = jnp.max(scores, axis=-1)
        expo = jnp.where(valid, jnp.exp(scores - block_max[..., None]), 0.0)
        block_total = jnp.sum(expo, axis=-1).reshape(rows, QH)
        block_acc = jnp.einsum(
            "rkgw,rwkd->rkgd",
            expo.astype(jnp.bfloat16),
            values4,
            preferred_element_type=jnp.float32,
        )
        block_acc = block_acc.reshape(rows, QH, HD)
        block_max = block_max.reshape(rows, QH)
        cache_top, cache_total, cache_acc = fold_sources(
            (
                lax.all_to_all(block_max[None], "tensor", split_axis=2, concat_axis=0, tiled=True),
                lax.all_to_all(
                    block_total[None], "tensor", split_axis=2, concat_axis=0, tiled=True
                ),
                lax.all_to_all(block_acc[None], "tensor", split_axis=2, concat_axis=0, tiled=True),
            )
        )
        query_own = query_part.reshape(rows, heads_dev, HD)
        fresh_k = jnp.take(jnp.stack(new_keys, axis=1), kv_index, axis=2)
        fresh_v = jnp.take(jnp.stack(new_values, axis=1), kv_index, axis=2)
        recent = (
            jnp.einsum("rhd,rjhd->rhj", query_own, fresh_k, preferred_element_type=jnp.float32)
            * scale
        )
        recent_max = jnp.max(recent, axis=-1)
        recent_exp = jnp.exp(recent - recent_max[..., None])
        recent_total = jnp.sum(recent_exp, axis=-1)
        recent_acc = jnp.einsum(
            "rhj,rjhd->rhd",
            recent_exp.astype(jnp.bfloat16),
            fresh_v,
            preferred_element_type=jnp.float32,
        )
        top = jnp.maximum(cache_top, recent_max)
        cache_factor = jnp.exp(cache_top - top)
        recent_factor = jnp.exp(recent_max - top)
        total = cache_factor * cache_total + recent_factor * recent_total
        acc = cache_factor[..., None] * cache_acc + recent_factor[..., None] * recent_acc
        attended = (acc / total[..., None]).astype(jnp.bfloat16).reshape(rows, heads_dev * HD)
        partial_out = jnp.dot(attended, w_out, preferred_element_type=jnp.float32)
        summed = lax.psum_scatter(partial_out, "tensor", scatter_dimension=1, tiled=True)
        outputs.append(summed.astype(jnp.bfloat16))
    return (reward, jnp.stack(outputs, axis=0))


def dot(a, b, dims=(((1,), (0,)), ((), ()))):
    return lax.dot_general(a, b, dims, preferred_element_type=jnp.float32)


def iota(shape, dim):
    return lax.broadcasted_iota(jnp.int32, shape, dim)


def kernel(
    n, ndp, rows, span, width,
    map_ref, len_ref, x_hbm, gain_ref, rgain_ref, rhead_ref, rh_hbm, wq_hbm, wkv_hbm, wo_hbm, k_hbm, v_hbm,
    reward_ref, out_ref,
    rh, wq, wkv, wo, kbuf, vbuf,
    xall, xg, normed, kvg, fresh, qf, qtmp, qsend, qg, accs, accr, mls, mlr, fac, att, osend, orecv, fin,
    rw, rwr, rwo,
    loc, xds, xdr, xs, xr, rs, rr, rbs, rbr, kvs, kvr, qs, qr, as_, ar, ms, mr, os_, or_, fds, fdr,
):
    me = lax.axis_index("tensor")
    dp = lax.axis_index("dp")
    other = 1 - dp
    feat = x_hbm.shape[1]
    pages = rows // 2
    per = 2 * STEPS
    R = rows * STEPS
    group = QH // KVH
    unit = group * per
    total_rows = pages * unit
    scale = HD ** (-0.5)

    def peer(k):
        return lax.rem(me + k, n)

    nz = n // 2
    y = lax.rem(me, 2)
    z = me // 2
    mate = me + 1 - 2 * y

    def ahead(k):
        return lax.rem(z + k, nz) * 2 + y

    def ahead_mate(k):
        return lax.rem(z + k, nz) * 2 + 1 - y

    def source(j):
        side = j // nz
        return lax.rem(z + nz - lax.rem(j, nz), nz) * 2 + y + side * (1 - 2 * y)

    copies = []

    def load(src, dst):
        c = pltpu.make_async_copy(src, dst, loc.at[len(copies)])
        c.start()
        copies.append(c)
        return c

    def load_rows(src, dst, parts):
        step = src.shape[0] // parts
        return [load(src.at[pl.ds(i * step, step)], dst.at[pl.ds(i * step, step)]) for i in range(parts)]

    c_x = load(x_hbm, xall.at[dp])
    c_rh = load_rows(rh_hbm, rh, 2)
    c_wq = load_rows(wq_hbm, wq, 4)

    barrier = pltpu.get_barrier_semaphore()
    for k in range(1, n):
        pl.semaphore_signal(barrier, inc=1, device_id={"tensor": peer(k)}, device_id_type=pl.DeviceIdType.MESH)
    pl.semaphore_signal(barrier, inc=1, device_id={"dp": other}, device_id_type=pl.DeviceIdType.MESH)

    def to_peer(k, src, dst, ssem, rsem):
        return pltpu.make_async_remote_copy(
            src_ref=src, dst_ref=dst, send_sem=ssem, recv_sem=rsem,
            device_id={"tensor": peer(k)}, device_id_type=pl.DeviceIdType.MESH,
        )

    def to_dev(dev, src, dst, ssem, rsem):
        return pltpu.make_async_remote_copy(
            src_ref=src, dst_ref=dst, send_sem=ssem, recv_sem=rsem,
            device_id={"tensor": dev}, device_id_type=pl.DeviceIdType.MESH,
        )

    def to_pair(src, dst, ssem, rsem):
        return pltpu.make_async_remote_copy(
            src_ref=src, dst_ref=dst, send_sem=ssem, recv_sem=rsem,
            device_id={"dp": other}, device_id_type=pl.DeviceIdType.MESH,
        )

    slot = [map_ref[s] for s in range(ndp * rows)]
    first, second = [], []
    for b in range(ndp):
        mine = [jnp.int32(b * rows)] * pages
        count = jnp.int32(0)
        for s in range(b * rows, (b + 1) * rows):
            kept = slot[s] == s
            for i in range(pages):
                mine[i] = jnp.where(kept & (count == i), s, mine[i])
            count = count + jnp.where(kept, 1, 0)
        first.append(mine)
        named = []
        for i in range(pages):
            found = jnp.int32(0)
            for s in range(ndp * rows):
                found = jnp.where((slot[s] == mine[i]) & (mine[i] != s), s, found)
            named.append(found)
        second.append(named)

    def own(lists, i):
        return jnp.where(dp == 0, lists[0][i], lists[1][i])

    first_own = [own(first, i) for i in range(pages)]
    second_own = [own(second, i) for i in range(pages)]

    c_x.wait()
    pl.semaphore_wait(barrier, n)
    pair_x = to_pair(xall.at[dp], xall.at[dp], xds.at[0], xdr.at[0])
    pair_x.start()

    r_i = iota((R, ndp * R), 0)
    c_i = iota((R, ndp * R), 1)
    row_slot = jnp.zeros((R, ndp * R), jnp.int32)
    for i in range(pages):
        row_slot = jnp.where(r_i // STEPS == 2 * i, first_own[i], row_slot)
        row_slot = jnp.where(r_i // STEPS == 2 * i + 1, second_own[i], row_slot)
    col_slot = (c_i // R) * rows + c_i % rows
    pick = (row_slot == col_slot) & (r_i % STEPS == (c_i % R) // rows)
    pick = jnp.where(pick, 1.0, 0.0).astype(jnp.bfloat16)

    pltpu.make_async_remote_copy(
        src_ref=xall.at[other], dst_ref=xall.at[other], send_sem=xds.at[0], recv_sem=xdr.at[0],
        device_id={"dp": other}, device_id_type=pl.DeviceIdType.MESH,
    ).wait_recv()
    chosen = dot(pick, xall[...].reshape(ndp * R, feat))
    xg[me] = chosen.astype(jnp.bfloat16)
    sends = [pair_x]
    for k in range(1, nz):
        c = to_dev(ahead(k), xg.at[me], xg.at[me], xs.at[k], xr.at[k])
        c.start()
        sends.append(c)
    c = to_dev(mate, xg.at[me], xg.at[me], xs.at[nz], xr.at[nz])
    c.start()
    sends.append(c)

    for c in c_rh:
        c.wait()
    weight = rgain_ref[...] * rhead_ref[...]

    def reward_step(r, carry):
        start = pl.multiple_of(r * span, span)
        square = jnp.zeros((span, 128), jnp.float32)
        head = jnp.zeros((span, 128), jnp.float32)
        for b in range(feat // 128):
            h = rh[pl.ds(start, span), b * 128 : (b + 1) * 128].astype(jnp.float32)
            square = square + h * h
            head = head + h * weight[:, b * 128 : (b + 1) * 128]
        rw[r, 0:1, :] = jnp.sum(jnp.transpose(square), axis=0, keepdims=True)
        rw[r, 1:2, :] = jnp.sum(jnp.transpose(head), axis=0, keepdims=True)
        return carry

    lax.fori_loop(0, rows // 2, reward_step, 0)
    for k in range(1, nz):
        s = source(k)
        to_dev(mate, xg.at[s], xg.at[s], xs.at[k], xr.at[k]).wait_recv()
        c = to_dev(mate, xg.at[s], xg.at[s], xs.at[nz + k], xr.at[nz + k])
        c.start()
        sends.append(c)
    lax.fori_loop(rows // 2, rows, reward_step, 0)
    for k in range(1, n):
        c = to_peer(k, rw.at[peer(k)], rwr.at[k], rs.at[k], rr.at[k])
        c.start()
        sends.append(c)
    rwr[0] = rw[me]

    mean = jnp.zeros((R, 1), jnp.float32)
    for j in range(nz, n):
        s = source(j)
        to_dev(mate, xg.at[s], xg.at[s], xs.at[j], xr.at[j]).wait_recv()
    for s in range(n):
        part = xg[s].astype(jnp.float32)
        mean = mean + jnp.sum(part * part, axis=1, keepdims=True)
    factor = lax.rsqrt(mean / (n * feat) + EPS)
    for s in range(n):
        lo, hi = s * feat, (s + 1) * feat
        part = xg[s].astype(jnp.float32)
        normed[:, lo:hi] = (part * factor * gain_ref[:, lo:hi]).astype(jnp.bfloat16)

    for c in c_wq:
        c.wait()
    c_wkv = load_rows(wkv_hbm, wkv, 2)
    c_k = load_rows(k_hbm, kbuf, 2)
    c_v = load_rows(v_hbm, vbuf, 2)
    c_wo = load_rows(wo_hbm, wo, 4)
    chunk = 256

    def query_step(c, carry):
        cols = pl.ds(pl.multiple_of(c * chunk, chunk), chunk)
        qf[:, cols] = dot(normed[...], wq[:, cols])
        return carry

    lax.fori_loop(0, group * HD // chunk, query_step, 0)
    for i in range(pages):
        for h in range(group):
            at = i * unit + h * per
            qtmp[at : at + per, :] = qf[i * per : (i + 1) * per, h * HD : (h + 1) * HD]
    qsend[...] = qtmp[...].astype(jnp.bfloat16)
    for k in range(1, nz):
        c = to_dev(ahead(k), qsend, qg.at[k], qs.at[k], qr.at[k])
        c.start()
        sends.append(c)
    c = to_dev(mate, qsend, qg.at[nz], qs.at[nz], qr.at[nz])
    c.start()
    sends.append(c)
    qg[0] = qsend[...]

    for c in c_wkv:
        c.wait()
    keyval = dot(normed[...], wkv[...]).astype(jnp.bfloat16)
    per_dev = wkv.shape[1] // HD
    kind = me * per_dev // KVH
    for p in range(per_dev):
        kvg[p] = keyval[:, p * HD : (p + 1) * HD]
        dest = lax.rem(me * per_dev + p, KVH)

        @pl.when(dest != me)
        def _():
            to_dev(dest, kvg.at[p], fresh.at[kind], kvs.at[p], kvr.at[kind]).start()

        @pl.when(dest == me)
        def _():
            fresh[kind] = kvg[p]


    for c in c_k + c_v:
        c.wait()
    live = [len_ref[first_own[i]] for i in range(pages)]
    page = [first_own[i] - dp * rows for i in range(pages)]
    place = me * width + iota((unit, width), 1)
    lane = iota((unit, HD), 1)

    def attend(k):
        cols = pl.ds(pl.multiple_of(source(k) * HD, HD), HD)
        packed = []
        for i in range(pages):
            q = qg[k, i * unit : (i + 1) * unit, :]
            valid = place < live[i]
            score = dot(q, kbuf[page[i], :, cols], (((1,), (1,)), ((), ()))) * scale
            score = jnp.where(valid, score, NEG)
            top = jnp.max(score, axis=1, keepdims=True)
            expo = jnp.where(valid, jnp.exp(score - top), 0.0)
            total = jnp.sum(expo, axis=1, keepdims=True)
            acc = dot(expo.astype(jnp.bfloat16), vbuf[page[i], :, cols])
            accs[k, i * unit : (i + 1) * unit, :] = acc.astype(jnp.bfloat16)
            packed.append(jnp.where(lane == 0, top, jnp.where(lane == 1, total, 0.0)))
        mls[k] = jnp.transpose(jnp.concatenate(packed, axis=0))[:8]

    def reply(k):
        dest = {"tensor": source(k)}
        return [
            pltpu.make_async_remote_copy(
                src_ref=accs.at[k], dst_ref=accr.at[k], send_sem=as_.at[k], recv_sem=ar.at[k],
                device_id=dest, device_id_type=pl.DeviceIdType.MESH,
            ),
            pltpu.make_async_remote_copy(
                src_ref=mls.at[k], dst_ref=mlr.at[k], send_sem=ms.at[k], recv_sem=mr.at[k],
                device_id=dest, device_id_type=pl.DeviceIdType.MESH,
            ),
        ]

    def arrived(j):
        to_dev(mate, qsend, qg.at[j], qs.at[j], qr.at[j]).wait_recv()

    def hand_on(k):
        return to_dev(mate, qg.at[k], qg.at[nz + k], qs.at[nz + k], qr.at[nz + k])

    def near_step(k, carry):
        arrived(k)
        hand_on(k).start()
        attend(k)
        for c in reply(k):
            c.start()
        return carry

    def far_step(j, carry):
        arrived(j)
        attend(j)
        for c in reply(j):
            c.start()
        return carry

    attend(0)
    lax.fori_loop(1, nz, near_step, 0)
    lax.fori_loop(nz, n, far_step, 0)

    for k in range(1, n):
        to_peer(k, rw.at[0], rwr.at[k], rs.at[k], rr.at[k]).wait_recv()
    sums = jnp.sum(rwr[...], axis=0)
    score = sums[1:2] * lax.rsqrt(sums[0:1] / (n * feat) + EPS)
    rwo[me] = jnp.broadcast_to(jnp.sum(score, axis=1, keepdims=True) / span, rwo.shape[1:])
    for k in range(1, n):
        c = to_peer(k, rwo.at[me], rwo.at[me], rbs.at[k], rbr.at[k])
        c.start()
        sends.append(c)

    for kd in range(2):
        origin = (me + kd * KVH) // per_dev

        @pl.when(origin != me)
        def _():
            to_dev(mate, kvg.at[0], fresh.at[kd], kvs.at[0], kvr.at[kd]).wait_recv()

    fresh_k = fresh[0]
    fresh_v = fresh[1]
    q_row = iota((total_rows, R), 0)
    k_row = iota((total_rows, R), 1)
    q_slot = (q_row // unit) * 2 + (q_row % per) // STEPS
    valid = (q_slot == k_row // STEPS) & (k_row % STEPS <= q_row % STEPS)
    score = dot(qsend[...], fresh_k, (((1,), (1,)), ((), ()))) * scale
    score = jnp.where(valid, score, NEG)
    new_top = jnp.max(score, axis=1, keepdims=True)
    expo = jnp.where(valid, jnp.exp(score - new_top), 0.0)
    new_total = jnp.sum(expo, axis=1, keepdims=True)
    new_acc = dot(expo.astype(jnp.bfloat16), fresh_v)
    lane = iota((total_rows, HD), 1)
    new_ml = jnp.transpose(jnp.where(lane == 0, new_top, jnp.where(lane == 1, new_total, 0.0)))

    for k in range(1, n):
        for c in reply(k):
            c.wait_recv()
    tops = [mls[0, 0:1, :]] + [mlr[k, 0:1, :] for k in range(1, n)] + [new_ml[0:1]]
    totals = [mls[0, 1:2, :]] + [mlr[k, 1:2, :] for k in range(1, n)] + [new_ml[1:2]]
    top = functools.reduce(jnp.maximum, tops)
    factors = [jnp.exp(t - top) for t in tops]
    whole = functools.reduce(jnp.add, [f * t for f, t in zip(factors, totals)])
    inverse = 1.0 / whole
    fac[...] = jnp.zeros_like(fac)
    for k in range(n + 1):
        fac[k : k + 1, :] = factors[k] * inverse
    turned = jnp.transpose(fac[...])
    folded = turned[:, n : n + 1] * new_acc + turned[:, 0:1] * accs[0].astype(jnp.float32)
    for k in range(1, n):
        folded = folded + turned[:, k : k + 1] * accr[k].astype(jnp.float32)
    qtmp[...] = folded
    for i in range(pages):
        for h in range(group):
            at = i * unit + h * per
            qf[i * per : (i + 1) * per, h * HD : (h + 1) * HD] = qtmp[at : at + per, :]
    att[...] = qf[...].astype(jnp.bfloat16)

    for c in c_wo:
        c.wait()

    def out_part(dev):
        return dot(att[...], wo[:, pl.ds(pl.multiple_of(dev * feat, feat), feat)])

    def mate_share(j):
        return to_dev(mate, osend.at[j], orecv.at[j], os_.at[j], or_.at[j])

    def pair_share(k):
        return to_dev(ahead(k), osend.at[k], orecv.at[k], os_.at[k], or_.at[k])

    def mate_step(i, carry):
        k = lax.rem(i, nz)
        osend[nz + k] = out_part(ahead_mate(k)).astype(jnp.bfloat16)
        mate_share(nz + k).start()
        return carry

    def pair_step(k, carry):
        share = out_part(ahead(k))
        mate_share(nz + k).wait_recv()
        osend[k] = (share + orecv[nz + k].astype(jnp.float32)).astype(jnp.bfloat16)
        pair_share(k).start()
        return carry

    lax.fori_loop(1, nz + 1, mate_step, 0)
    lax.fori_loop(1, nz, pair_step, 0)
    qf[...] = out_part(me)
    summed = qf[...]
    mate_share(nz).wait_recv()
    summed = summed + orecv[nz].astype(jnp.float32)
    for k in range(1, nz):
        pair_share(k).wait_recv()
        summed = summed + orecv[k].astype(jnp.float32)
    fin[dp] = summed.astype(jnp.bfloat16)
    pair_f = to_pair(fin.at[dp], fin.at[dp], fds.at[0], fdr.at[0])
    pair_f.start()
    sends.append(pair_f)

    virtual = jnp.zeros((R, ndp * R), jnp.int32)
    for b in range(ndp):
        for i in range(pages):
            at = b * rows + 2 * i
            virtual = jnp.where(c_i // STEPS == at, first[b][i], virtual)
            virtual = jnp.where(c_i // STEPS == at + 1, second[b][i], virtual)
    place_back = (virtual == dp * rows + r_i % rows) & (c_i % STEPS == r_i // rows)
    place_back = jnp.where(place_back, 1.0, 0.0).astype(jnp.bfloat16)
    pltpu.make_async_remote_copy(
        src_ref=fin.at[other], dst_ref=fin.at[other], send_sem=fds.at[0], recv_sem=fdr.at[0],
        device_id={"dp": other}, device_id_type=pl.DeviceIdType.MESH,
    ).wait_recv()
    out_ref[...] = dot(place_back, fin[...].reshape(ndp * R, feat)).astype(jnp.bfloat16)

    result = jnp.zeros((1, rows), jnp.float32)
    for k in range(1, n):
        dev = source(k)
        to_peer(k, rwo.at[me], rwo.at[dev], rbs.at[k], rbr.at[k]).wait_recv()
    for r in range(rows):
        result = jnp.where(iota((1, rows), 1) == r, rwo[r, 0:1, 0:rows], result)
    reward_ref[...] = result

    for c in sends:
        c.wait_send()
    for p in range(per_dev):
        dest = lax.rem(me * per_dev + p, KVH)

        @pl.when(dest != me)
        def _():
            to_dev(dest, kvg.at[p], fresh.at[kind], kvs.at[p], kvr.at[kind]).wait_send()

    for k in range(1, n):
        for c in reply(k):
            c.wait_send()
    for k in range(1, nz):
        hand_on(k).wait_send()
        pair_share(k).wait_send()
    for j in range(nz, n):
        mate_share(j).wait_send()


def write_results(reward_in, out_in, reward_ref, out_ref, sem):
    copies = [
        pltpu.make_async_copy(reward_in, reward_ref, sem.at[0]),
        pltpu.make_async_copy(out_in, out_ref, sem.at[1]),
    ]
    for c in copies:
        c.start()
    for c in copies:
        c.wait()


def fused(
    n, ndp,
    reward_hidden, reward_gain, reward_head, decode_inputs, attn_gain, w_query, w_keyval, w_out,
    cache_keys, cache_values, lengths, slot_map,
):
    rows, span, feat = reward_hidden.shape
    width = cache_keys.shape[1]
    R = STEPS * rows
    cols = w_query.shape[1]
    kv_cols = w_keyval.shape[1]
    bf, f32 = jnp.bfloat16, jnp.float32
    total_rows = rows * STEPS * (QH // KVH)
    big = [
        pltpu.VMEM((rows * span, feat), bf),
        pltpu.VMEM(w_query.shape, bf),
        pltpu.VMEM(w_keyval.shape, bf),
        pltpu.VMEM(w_out.shape, bf),
        pltpu.VMEM(cache_keys.shape, bf),
        pltpu.VMEM(cache_values.shape, bf),
    ]
    small = [
        pltpu.VMEM((ndp, R, feat), bf),
        pltpu.VMEM((n, R, feat), bf),
        pltpu.VMEM((R, n * feat), bf),
        pltpu.VMEM((kv_cols // HD, R, HD), bf),
        pltpu.VMEM((2, R, HD), bf),
        pltpu.VMEM((R, cols), f32),
        pltpu.VMEM((total_rows, HD), f32),
        pltpu.VMEM((total_rows, HD), bf),
        pltpu.VMEM((n, total_rows, HD), bf),
        pltpu.VMEM((n, total_rows, HD), bf),
        pltpu.VMEM((n, total_rows, HD), bf),
        pltpu.VMEM((n, 8, total_rows), f32),
        pltpu.VMEM((n, 8, total_rows), f32),
        pltpu.VMEM((HD, total_rows), f32),
        pltpu.VMEM((R, cols), bf),
        pltpu.VMEM((n, R, feat), bf),
        pltpu.VMEM((n, R, feat), bf),
        pltpu.VMEM((ndp, R, feat), bf),
        pltpu.VMEM((rows, 2, span), f32),
        pltpu.VMEM((n, 2, span), f32),
        pltpu.VMEM((rows, 8, 128), f32),
    ]
    sem = pltpu.SemaphoreType.DMA
    sems = [sem((17,)), sem((1,)), sem((1,))] + [sem((n,)) for _ in range(16)] + [sem((1,)), sem((1,))]
    vmem, smem, hbm = (pl.BlockSpec(memory_space=m) for m in (pltpu.VMEM, pltpu.SMEM, pl.ANY))
    reward, out = pl.pallas_call(
        functools.partial(kernel, n, ndp, rows, span, width),
        out_shape=(jax.ShapeDtypeStruct((1, rows), f32), jax.ShapeDtypeStruct((R, feat), bf)),
        in_specs=[smem, smem, hbm, vmem, vmem, vmem] + [hbm] * 6,
        out_specs=(vmem, vmem),
        scratch_shapes=big + small + sems,
        compiler_params=pltpu.CompilerParams(
            collective_id=0, has_side_effects=True, vmem_limit_bytes=60 * 2**20
        ),
        name="prune_and_decode",
    )(
        slot_map,
        lengths,
        decode_inputs.reshape(R, feat),
        attn_gain.reshape(1, -1),
        reward_gain.reshape(1, -1),
        reward_head.reshape(1, -1),
        reward_hidden.reshape(rows * span, feat),
        w_query,
        w_keyval,
        w_out,
        cache_keys,
        cache_values,
    )
    reward, out = pl.pallas_call(
        write_results,
        out_shape=(jax.ShapeDtypeStruct((1, rows), f32), jax.ShapeDtypeStruct((R, feat), bf)),
        in_specs=[hbm, hbm],
        out_specs=(hbm, hbm),
        scratch_shapes=[sem((2,))],
        name="write_results",
    )(reward, out)
    return reward.reshape(rows), out.reshape(STEPS, rows, feat)


def device_program(mesh):
    n, ndp = mesh.shape["tensor"], mesh.shape["dp"]

    def run(*args):
        if n == KVH and ndp == 2 and args[0].shape[0] == n:
            return fused(n, ndp, *args)
        return local(*args)

    return run


def solution(mesh):
    return jax.shard_map(
        device_program(mesh),
        mesh=mesh,
        in_specs=(
            P(("groups", "dp"), None, "tensor"),
            P("tensor"),
            P("tensor"),
            P(None, ("groups", "dp"), "tensor"),
            P(),
            P(None, "tensor"),
            P(None, "tensor"),
            P("tensor", None),
            P(("groups", "dp"), "tensor", None),
            P(("groups", "dp"), "tensor", None),
            P("groups"),
            P("groups"),
        ),
        out_specs=(P(("groups", "dp")), P(None, ("groups", "dp"), "tensor")),
        check_vma=False,
    )
```
